32 devices in a mesh: dp: 8 (over y, x, core), tensor: 4 (over z).
Axes of the slice: x: 2, y: 2, z: 4, core: 2. Of those that a mesh axis runs over, the one named last changes fastest.
Arguments:
- tokens: bfloat16 [8, 4, 256, 1024], P('dp', None, 'tensor'), may hold values from -6 to 6
- cotangent: bfloat16 [8, 4, 256, 1024], P('dp', None, 'tensor'), may hold values from -6 to 6
- lengths: int32 [16], replicated, may hold values from 1 to 1024, as said below
- groups: int32 [16], replicated, may hold values from 0 to 7, as said below
- offsets: int32 [16], replicated, may hold values from 0 to 7
- attention_gain: float32 [1024], replicated, may hold values from 0.25 to 1.75
- feed_gain: float32 [1024], replicated, may hold values from 0.25 to 1.75
- query_gain: float32 [64], replicated, may hold values from 0.25 to 1.75
- key_gain: float32 [64], replicated, may hold values from 0.25 to 1.75
- query_weight: bfloat16 [1024, 1024], P('dp', 'tensor'), may hold values from -0.1875 to 0.1875
- key_weight: bfloat16 [1024, 512], P('dp', 'tensor'), may hold values from -0.1875 to 0.1875
- value_weight: bfloat16 [1024, 512], P('dp', 'tensor'), may hold values from -0.1875 to 0.1875
- out_weight: bfloat16 [1024, 1024], P('tensor', 'dp'), may hold values from -3 to 3
- gate_weight: bfloat16 [1024, 4608], P('dp', 'tensor'), may hold values from -0.1875 to 0.1875
- up_weight: bfloat16 [1024, 4608], P('dp', 'tensor'), may hold values from -0.1875 to 0.1875
- down_weight: bfloat16 [4608, 1024], P('tensor', 'dp'), may hold values from -0.09375 to 0.09375
Outputs:
- output: bfloat16 [8, 4, 256, 1024], P('dp', None, 'tensor')
- grad_tokens: bfloat16 [8, 4, 256, 1024], P('dp', None, 'tensor')
- grad_attention_gain: float32 [1024], replicated
- grad_feed_gain: float32 [1024], replicated
- grad_query_gain: float32 [64], replicated
- grad_key_gain: float32 [64], replicated
- grad_query_weight: float32 [1024, 1024], P('dp', 'tensor')
- grad_key_weight: float32 [1024, 512], P('dp', 'tensor')
- grad_value_weight: float32 [1024, 512], P('dp', 'tensor')
- grad_out_weight: float32 [1024, 1024], P('tensor', 'dp')
- grad_gate_weight: float32 [1024, 4608], P('dp', 'tensor')
- grad_up_weight: float32 [1024, 4608], P('dp', 'tensor')
- grad_down_weight: float32 [4608, 1024], P('tensor', 'dp')
The draws below stay inside these ranges and needn't reach their ends.
Inputs may be any that keep to these rules, and one draw needn't show every extreme that they name: `lengths`: each sequence lies inside its dp index's 1024 rows, starts on a block and intersections no other; some sequence has exactly 1024 tokens. `groups`: each dp index holds one or three sequences.
All inputs are finite; a program needn't handle non-finite values.
Results may differ from the reference program's by a relative error of at most 0.018.
Values may be sent and summed in bfloat16 or wider, within the bound.
No kernel may reach another device: no remote copies, remote signals or barrier semaphores. Data moves between devices by JAX's collectives and lax.ppermute only.
A program may use at most 128 MiB of HBM per device.

```python
import jax
import jax.numpy as jnp
from jax import lax

D = 1024
H = 16
KVH = 8
HD = 64
FF = 4608
BLOCK = 128
UNIT = 64
MAXLEN = 1024
GRP_BLOCKS = 8
UNITS_DEV = 4
SEQS = 16
N_DP = 8
N_TENSOR = 4


def packing(key):
    half = N_DP // 2
    most_blocks = MAXLEN // BLOCK
    span_blocks = N_TENSOR * UNIT // BLOCK
    order = jax.random.permutation(jax.random.fold_in(key, 11), N_DP).astype(jnp.int32)
    rank = jnp.argsort(order, stable=True).astype(jnp.int32)
    three = rank < half
    top_first = jnp.where(three, min(most_blocks, GRP_BLOCKS - 2), min(most_blocks, GRP_BLOCKS))
    first_blocks = jax.random.randint(jax.random.fold_in(key, 12), (N_DP,), span_blocks, top_first + 1)
    longest = rank == N_DP - 1
    first_blocks = jnp.where(longest, most_blocks, first_blocks)
    rest = GRP_BLOCKS - first_blocks
    top_second = jnp.maximum(jnp.minimum(rest - 1, most_blocks), 1)
    second_blocks = jax.random.randint(jax.random.fold_in(key, 13), (N_DP,), 1, top_second + 1)
    top_third = jnp.maximum(jnp.minimum(rest - second_blocks, most_blocks), 1)
    third_blocks = jax.random.randint(jax.random.fold_in(key, 14), (N_DP,), 1, top_third + 1)
    tail_first = jax.random.randint(jax.random.fold_in(key, 15), (N_DP,), 1, BLOCK + 1)
    tail_first = jnp.where(longest, BLOCK, tail_first)
    tail_second = jax.random.randint(jax.random.fold_in(key, 16), (N_DP,), 1, BLOCK + 1)
    tail_third = jax.random.randint(jax.random.fold_in(key, 17), (N_DP,), 1, BLOCK + 1)
    chosen = order[:half]
    lengths = jnp.concatenate([(first_blocks - 1) * BLOCK + tail_first, ((second_blocks - 1) * BLOCK + tail_second)[chosen], ((third_blocks - 1) * BLOCK + tail_third)[chosen]])
    groups = jnp.concatenate([jnp.arange(N_DP, dtype=jnp.int32), chosen, chosen])
    offsets = jnp.concatenate([jnp.zeros((N_DP,), jnp.int32), first_blocks[chosen], (first_blocks + second_blocks)[chosen]])
    return (lengths.astype(jnp.int32), groups.astype(jnp.int32), offsets.astype(jnp.int32))


def draw_lengths(key, part):
    shared = packing(key)
    return shared[0]


def draw_groups(key, part):
    shared = packing(key)
    return shared[1]


def draw_offsets(key, part):
    shared = packing(key)
    return shared[2]


def block_levels(stream_key, dims, shards, smallest, largest):
    loudness, own = 1.0, jax.random.fold_in(stream_key, 6)
    for dim, parts in shards:
        draws = jnp.exp(jax.random.uniform(jax.random.fold_in(own, dim), (parts,), jnp.float32, smallest / len(shards), largest / len(shards)))
        loudness = loudness * jnp.repeat(draws, dims[dim] // parts).reshape([-1 if axis == dim else 1 for axis in range(len(dims))])
    return loudness


def gaussian(key, shape, width, reach, cuts=(), kind=jnp.bfloat16):
    drawn = width * jax.random.normal(key, shape, jnp.float32)
    if cuts:
        drawn = drawn * block_levels(key, shape, cuts, -0.22, 0.18)
    return jnp.clip(drawn, -reach, reach).astype(kind)


def setup_inputs(seed: int = 0) -> dict:
    splits = jax.random.split(jax.random.key(seed), 17)
    return {
        "tokens": gaussian(splits[0], (N_DP, UNITS_DEV, N_TENSOR * UNIT, D), 1.0, 6.0, ((0, 8), (2, 4))),
        "cotangent": gaussian(splits[1], (N_DP, UNITS_DEV, N_TENSOR * UNIT, D), 1.0, 6.0, ((0, 8), (2, 4))),
        "lengths": draw_lengths(jax.random.fold_in(splits[16], 71), 0),
        "groups": draw_groups(jax.random.fold_in(splits[16], 71), 0),
        "offsets": draw_offsets(jax.random.fold_in(splits[16], 71), 0),
        "attention_gain": jnp.clip(1.0 + 0.15 * jax.random.normal(splits[5], (D,), jnp.float32), 0.25, 1.75),
        "feed_gain": jnp.clip(1.0 + 0.15 * jax.random.normal(splits[6], (D,), jnp.float32), 0.25, 1.75),
        "query_gain": jnp.clip(1.0 + 0.15 * jax.random.normal(splits[7], (HD,), jnp.float32), 0.25, 1.75),
        "key_gain": jnp.clip(1.0 + 0.15 * jax.random.normal(splits[8], (HD,), jnp.float32), 0.25, 1.75),
        "query_weight": gaussian(splits[9], (D, H * HD), D ** -0.5, 0.1875, ((0, 8), (1, 4))),
        "key_weight": gaussian(splits[10], (D, KVH * HD), D ** -0.5, 0.1875, ((0, 8), (1, 4))),
        "value_weight": gaussian(splits[11], (D, KVH * HD), D ** -0.5, 0.1875, ((0, 8), (1, 4))),
        "out_weight": gaussian(splits[12], (H * HD, D), (max(H * HD // 256, 1)) ** -0.5, 3.0, ((0, 4), (1, 8))),
        "gate_weight": gaussian(splits[13], (D, FF), D ** -0.5, 0.1875, ((0, 8), (1, 4))),
        "up_weight": gaussian(splits[14], (D, FF), D ** -0.5, 0.1875, ((0, 8), (1, 4))),
        "down_weight": gaussian(splits[15], (FF, D), FF ** -0.5, 0.09375, ((0, 4), (1, 8))),
    }


EPS = 1e-05
THETA = 1000000.0
NEG = -1e+30
HIGHEST = lax.Precision.HIGHEST

@jax.custom_vjp
def low(v):
    return lax.optimization_barrier(v.astype(jnp.bfloat16)).astype(jnp.float32)

@jax.custom_vjp
def low_back(v):
    return v

def low_keep(v):
    return (low(v), None)

def low_pass(kept, grad):
    return (grad,)

def back_keep(v):
    return (v, None)

def back_low(kept, grad):
    return (low(grad),)
low.defvjp(low_keep, low_pass)
low_back.defvjp(back_keep, back_low)

def matmul(left, right):
    return jnp.dot(left, right, precision=HIGHEST)

def norm_rows(values, gain):
    return values * lax.rsqrt(lax.optimization_barrier(jnp.mean(values * values, axis=-1, keepdims=True)) + EPS) * gain

def turn_half(values):
    half = values.shape[-1] // 2
    return jnp.concatenate([-values[..., half:], values[..., :half]], axis=-1)

def rotated(values, gain, cosine, sine):
    normed = norm_rows(values, gain)
    return normed * cosine + turn_half(normed) * sine

def layout(lengths, groups, offsets):
    position = jnp.arange(GRP_BLOCKS * BLOCK, dtype=jnp.int32)
    start = offsets * BLOCK
    finish = start + lengths
    number = jnp.arange(SEQS, dtype=jnp.int32)
    owner = jnp.arange(N_DP, dtype=jnp.int32)
    inside = ((groups[None, None, :] == owner[:, None, None]) & (position[None, :, None] >= start[None, None, :]) & (position[None, :, None] < finish[None, None, :])).astype(jnp.int32)
    segment = lax.optimization_barrier(jnp.sum(inside * (number + 1)[None, None, :], axis=-1)) - 1
    segment = jnp.where(segment >= 0, segment, -1 - position[None, :])
    inner_pos = lax.optimization_barrier(jnp.sum(inside * (position[None, :, None] - start[None, None, :]), axis=-1))
    return (segment, inner_pos)

def group_forward(x, segment, inner_pos, weights):
    attention_gain, feed_gain, query_gain, key_gain, query_weight, key_weight, value_weight, out_weight, gate_weight, up_weight, down_weight = weights
    row_count = x.shape[0]
    head_dim = query_gain.shape[0]
    heads = query_weight.shape[1] // head_dim
    value_heads = key_weight.shape[1] // head_dim
    freq = THETA ** (-(jnp.arange(head_dim // 2, dtype=jnp.float32) * 2.0) / head_dim)
    angle = inner_pos.astype(jnp.float32)[:, None] * freq[None, :]
    cosine = jnp.concatenate([jnp.cos(angle), jnp.cos(angle)], axis=1)[:, None, :]
    sine = jnp.concatenate([jnp.sin(angle), jnp.sin(angle)], axis=1)[:, None, :]
    attn_rows = low(norm_rows(x, attention_gain))
    query_pre = low_back(matmul(attn_rows, query_weight)).reshape(row_count, heads, head_dim)
    key_pre = low_back(matmul(attn_rows, key_weight)).reshape(row_count, value_heads, head_dim)
    values = low(low_back(matmul(attn_rows, value_weight))).reshape(row_count, value_heads, head_dim)
    queries = low(rotated(query_pre, query_gain, cosine, sine)).reshape(row_count, value_heads, heads // value_heads, head_dim)
    keys = low(rotated(key_pre, key_gain, cosine, sine))
    scale = head_dim ** (-0.5)
    scores = low_back(jnp.einsum('qkgd,pkd->kgqp', queries, keys, precision=HIGHEST) * scale)
    position = jnp.arange(row_count, dtype=jnp.int32)
    allowed = (segment[:, None] == segment[None, :]) & (position[None, :] <= position[:, None])
    scores = jnp.where(allowed, scores, NEG)
    attend = jax.nn.softmax(scores, axis=-1)
    mixed = jnp.einsum('kgqp,pkd->qkgd', low(attend), values, precision=HIGHEST).reshape(row_count, heads * head_dim)
    mixed = low(low_back(mixed))
    branch = low_back(matmul(mixed, out_weight))
    middle = x + branch
    feed_rows = low(norm_rows(middle, feed_gain))
    gate = low_back(matmul(feed_rows, gate_weight))
    up = low_back(matmul(feed_rows, up_weight))
    hidden = low(jax.nn.silu(gate) * up)
    return middle + matmul(hidden, down_weight)

def forward_all(segment, inner_pos, tokens, weights):
    grouped = tokens.reshape(N_DP, GRP_BLOCKS * BLOCK, tokens.shape[-1])
    stepper = jax.checkpoint(group_forward)

    def advance(carry, inputs):
        return (carry, stepper(inputs[0], inputs[1], inputs[2], weights))
    _, result = lax.scan(advance, jnp.zeros((), jnp.float32), (grouped, segment, inner_pos))
    return result.reshape(tokens.shape)

def reference(tokens, cotangent, lengths, groups, offsets, attention_gain, feed_gain, query_gain, key_gain, query_weight, key_weight, value_weight, out_weight, gate_weight, up_weight, down_weight):
    segment, inner_pos = layout(lengths, groups, offsets)
    floats = [array.astype(jnp.float32) for array in (tokens, attention_gain, feed_gain, query_gain, key_gain, query_weight, key_weight, value_weight, out_weight, gate_weight, up_weight, down_weight)]

    def whole(*arrays):
        return forward_all(segment, inner_pos, arrays[0], tuple(arrays[1:]))
    output, pull = jax.vjp(whole, *floats)
    grads = pull(cotangent.astype(jnp.float32))
    return (output.astype(jnp.bfloat16), grads[0].astype(jnp.bfloat16), grads[1], grads[2], grads[3], grads[4], grads[5], grads[6], grads[7], grads[8], grads[9], grads[10], grads[11])
```

```python
import jax
import jax.numpy as jnp
from jax import lax
from jax.sharding import PartitionSpec as P

BLOCK = 128
QROWS = 512


EPS = 1e-05
THETA = 1000000.0
NEG = -1e30


def norm_rows(values, gain):
    return values * lax.rsqrt(jnp.mean(values * values, axis=-1, keepdims=True) + EPS) * gain


def norm_pull(values, gain, grad):
    inverse = lax.rsqrt(jnp.mean(values * values, axis=-1, keepdims=True) + EPS)
    scaled = grad * gain
    inner = jnp.mean(values * scaled, axis=-1, keepdims=True)
    grad_values = inverse * scaled - values * (inverse * inverse * inverse * inner)
    return grad_values, jnp.sum(grad * values * inverse, axis=0)


def turn_half(values):
    half = values.shape[-1] // 2
    return jnp.concatenate([-values[..., half:], values[..., :half]], axis=-1)


def rotated(values, gain, cosine, sine):
    normed = norm_rows(values, gain)
    return normed * cosine + turn_half(normed) * sine


def swap(values, axis, bit):
    count = lax.axis_size(axis)
    return lax.ppermute(values, axis, [(index, index ^ bit) for index in range(count)])


def bits_of(count):
    bits = []
    bit = 1
    while bit < count:
        bits.append(bit)
        bit *= 2
    return bits


def dot(left, right):
    return jnp.dot(left, right, preferred_element_type=jnp.float32)


def dot_t(left, right):
    return lax.dot_general(
        left, right, (((1,), (1,)), ((), ())), preferred_element_type=jnp.float32
    )


def dot_tl(left, right):
    return lax.dot_general(
        left, right, (((0,), (0,)), ((), ())), preferred_element_type=jnp.float32
    )


def spread(pieces, axis, bits):
    pieces = dict(pieces)
    for bit in bits:
        for key in sorted(pieces):
            pieces[key | bit] = swap(pieces[key], axis, bit)
    return pieces


def fold(pieces, axis, bits):
    pieces = dict(pieces)
    for bit in bits:
        for key in sorted(pieces, reverse=True):
            if key & bit:
                got = swap(pieces.pop(key).astype(jnp.bfloat16), axis, bit)
                pieces[key ^ bit] = pieces[key ^ bit] + got.astype(jnp.float32)
    return pieces


def place(pieces, index, dim, count):
    first = pieces[0]
    shape = list(first.shape)
    size = shape[dim]
    shape[dim] = size * count
    whole = jnp.zeros(shape, first.dtype)
    for key, block in pieces.items():
        whole = lax.dynamic_update_slice_in_dim(whole, block, (index ^ key) * size, dim)
    return whole


def cut(whole, index, dim, count, keys):
    size = whole.shape[dim] // count
    return {
        key: lax.dynamic_slice_in_dim(whole, (index ^ key) * size, size, dim) for key in keys
    }


def on_device(
    tokens,
    cotangent,
    lengths,
    groups,
    offsets,
    attention_gain,
    feed_gain,
    query_gain,
    key_gain,
    query_weight,
    key_weight,
    value_weight,
    out_weight,
    gate_weight,
    up_weight,
    down_weight,
):
    shard_shape = tokens.shape
    units, unit, width = shard_shape[1:]
    tensor_count = lax.axis_size("tensor")
    dp_count = lax.axis_size("dp")
    tensor_at = lax.axis_index("tensor")
    group = lax.axis_index("dp")
    first_core = (group & 1) == 0
    far = tensor_count // 2
    local_rows = units * unit
    group_rows = local_rows * tensor_count
    head_dim = query_gain.shape[0]
    tensor_bits = bits_of(tensor_count)
    near_bits = tensor_bits[:-1]
    dp_bits = bits_of(dp_count)
    plane_bits = dp_bits[1:]
    plane_back = plane_bits[::-1]
    low = jnp.bfloat16

    def rows_of_group(block):
        pieces = spread({0: block.reshape(units, unit, width)}, "tensor", tensor_bits[::-1])
        return place(pieces, tensor_at, 1, tensor_count).reshape(group_rows, width)

    def sum_to_rows(make):
        pieces = {key: make(key) for key in range(tensor_count - 1, -1, -1)}
        return fold(pieces, "tensor", tensor_bits)[0]

    def group_slice(whole, key):
        cube = whole.reshape(units, unit * tensor_count, whole.shape[-1])
        part = lax.dynamic_slice_in_dim(cube, (tensor_at ^ key) * unit, unit, 1)
        return part.reshape(local_rows, whole.shape[-1])

    def feed_spread(block):
        pieces = spread({0: block}, "tensor", near_bits[::-1])
        both = {2 * key: piece for key, piece in pieces.items()}
        for key in sorted(both):
            both[key | 1] = swap(both[key], "dp", 1)
        return jnp.concatenate([both[key] for key in sorted(both)], axis=0)

    def feed_fold(make):
        pieces = {key: make(key) for key in range(2 * far - 1, -1, -1)}
        pieces = fold(pieces, "dp", [1])
        pieces = {key // 2: piece for key, piece in pieces.items()}
        return fold(pieces, "tensor", near_bits)[0]

    def feed_weight(shard, dim, order):
        other = swap(shard, "tensor", far)
        keep = jnp.where(first_core, shard, other)
        got = swap(jnp.where(first_core, other, shard), "dp", 1)
        pieces = spread({0: keep, 1: got}, "dp", order)
        return place(pieces, group, dim, dp_count)

    def feed_weight_grad(whole, dim, order):
        pieces = cut(whole, group, dim, dp_count, range(dp_count))
        pieces = fold(pieces, "dp", order)
        got = swap(pieces[1].astype(low), "dp", 1).astype(jnp.float32)
        mine = jnp.where(first_core, pieces[0], got)
        away = jnp.where(first_core, got, pieces[0]).astype(low)
        return mine + swap(away, "tensor", far).astype(jnp.float32)

    def plane_weight(shard, dim, order):
        return place(spread({0: shard}, "dp", order + [1]), group, dim, dp_count)

    def plane_weight_grad(whole, dim, order):
        pieces = cut(whole, group, dim, dp_count, range(dp_count))
        return fold(pieces, "dp", [1] + order)[0]

    local_x = tokens.reshape(local_rows, width).astype(jnp.float32)
    attn_rows = rows_of_group(norm_rows(local_x, attention_gain).astype(low))
    query_cols = query_weight.shape[1]
    key_cols = key_weight.shape[1]
    heads = query_cols // head_dim
    value_heads = key_cols // head_dim
    repeat = heads // value_heads
    hidden_cols = gate_weight.shape[1]
    half_hidden = hidden_cols // 2
    project = plane_weight(
        jnp.concatenate([query_weight, key_weight, value_weight], axis=1), 0, plane_bits
    )
    out_full = plane_weight(out_weight, 1, plane_back)
    gate_full = feed_weight(gate_weight, 0, plane_bits)
    up_full = feed_weight(up_weight, 0, plane_back)
    down_full = jnp.concatenate(
        [
            feed_weight(down_weight[:half_hidden], 1, plane_bits),
            feed_weight(down_weight[half_hidden:], 1, plane_back),
        ],
        axis=0,
    )
    local_back = cotangent.reshape(local_rows, width)
    back_rows = feed_spread(local_back)

    position = jnp.arange(group_rows, dtype=jnp.int32)
    start = offsets * BLOCK
    finish = start + lengths
    number = jnp.arange(lengths.shape[0], dtype=jnp.int32)
    inside = (
        (groups[None, :] == group)
        & (position[:, None] >= start[None, :])
        & (position[:, None] < finish[None, :])
    ).astype(jnp.int32)
    segment = jnp.sum(inside * (number + 1)[None, :], axis=1) - 1
    segment = jnp.where(segment >= 0, segment, -1 - position)
    inner_pos = jnp.sum(inside * (position[:, None] - start[None, :]), axis=1)
    freq = THETA ** (-(jnp.arange(head_dim // 2, dtype=jnp.float32) * 2.0) / head_dim)
    angle = inner_pos.astype(jnp.float32)[:, None] * freq[None, :]
    cosine = jnp.concatenate([jnp.cos(angle), jnp.cos(angle)], axis=1)[:, None, :]
    sine = jnp.concatenate([jnp.sin(angle), jnp.sin(angle)], axis=1)[:, None, :]

    projected = dot(attn_rows, project)
    query_pre = projected[:, :query_cols].reshape(group_rows, heads, head_dim)
    key_pre = projected[:, query_cols : query_cols + key_cols].reshape(
        group_rows, value_heads, head_dim
    )
    value_pre = projected[:, query_cols + key_cols :]
    queries = (
        rotated(query_pre, query_gain, cosine, sine)
        .astype(jnp.bfloat16)
        .reshape(group_rows, value_heads, repeat, head_dim)
    )
    keys = rotated(key_pre, key_gain, cosine, sine).astype(jnp.bfloat16)
    values = value_pre.astype(jnp.bfloat16).reshape(group_rows, value_heads, head_dim)
    scale = head_dim ** (-0.5)
    block_count = group_rows // QROWS

    def block_scores(index):
        first = index * QROWS
        last = first + QROWS
        scores = (
            jnp.einsum(
                "qkgd,pkd->kgqp",
                queries[first:last],
                keys[:last],
                preferred_element_type=jnp.float32,
            )
            * scale
        )
        allowed = (segment[first:last, None] == segment[None, :last]) & (
            position[None, :last] <= position[first:last, None]
        )
        return jnp.where(allowed, scores, NEG)

    mixed_parts = []
    log_totals = []
    for index in range(block_count):
        last = (index + 1) * QROWS
        scores = block_scores(index)
        summit = jnp.max(scores, axis=-1, keepdims=True)
        shifted = jnp.exp(scores - summit)
        total = jnp.sum(shifted, axis=-1, keepdims=True)
        attend = (shifted / total).astype(jnp.bfloat16)
        log_totals.append(summit + jnp.log(total))
        mixed_parts.append(
            jnp.einsum("kgqp,pkd->qkgd", attend, values[:last], preferred_element_type=jnp.float32)
        )
    mixed = (
        jnp.concatenate(mixed_parts, axis=0)
        .reshape(group_rows, heads * head_dim)
        .astype(jnp.bfloat16)
    )
    attn_out = sum_to_rows(lambda key: dot(group_slice(mixed, key), out_full))
    middle = local_x + attn_out
    feed_rows = feed_spread(norm_rows(middle, feed_gain).astype(low))
    gate = dot(feed_rows, gate_full)
    up = dot(feed_rows, up_full)
    grad_hidden = dot_t(back_rows, down_full)
    sigmoid = jax.nn.sigmoid(gate)
    silu = gate * sigmoid
    hidden = (silu * up).astype(low)
    grad_gate = (grad_hidden * up * sigmoid * (1.0 + gate * (1.0 - sigmoid))).astype(low)
    grad_up = (grad_hidden * silu).astype(low)

    def block_of(whole, key):
        return lax.slice_in_dim(whole, key * local_rows, (key + 1) * local_rows, axis=0)

    grad_feed_in = feed_fold(
        lambda key: dot_t(block_of(grad_gate, key), gate_full)
        + dot_t(block_of(grad_up, key), up_full)
    )
    feed_out = feed_fold(lambda key: dot(block_of(hidden, key), down_full))
    output = (middle + feed_out).astype(low).reshape(shard_shape)
    grad_middle_norm, grad_feed_gain = norm_pull(middle, feed_gain, grad_feed_in)
    grad_middle = local_back.astype(jnp.float32) + grad_middle_norm
    back_attn = rows_of_group(grad_middle.astype(low))
    grad_gate_w = feed_weight_grad(dot_tl(feed_rows, grad_gate).astype(low), 0, plane_bits)
    grad_up_w = feed_weight_grad(dot_tl(feed_rows, grad_up).astype(low), 0, plane_back)
    grad_down = dot_tl(hidden, back_rows).astype(low)
    grad_down_w = jnp.concatenate(
        [
            feed_weight_grad(grad_down[:half_hidden], 1, plane_bits),
            feed_weight_grad(grad_down[half_hidden:], 1, plane_back),
        ],
        axis=0,
    )
    grad_out_w = plane_weight_grad(dot_tl(mixed, back_attn).astype(low), 1, plane_back)
    grad_mixed = (
        dot_t(back_attn, out_full)
        .astype(low)
        .reshape(group_rows, value_heads, repeat, head_dim)
    )
    grad_keys = jnp.zeros((group_rows, value_heads, head_dim), jnp.float32)
    grad_values = jnp.zeros((group_rows, value_heads, head_dim), jnp.float32)
    query_parts = []
    for index in range(block_count):
        first = index * QROWS
        last = first + QROWS
        scores = block_scores(index)
        attend = jnp.exp(scores - log_totals[index])
        attend_low = attend.astype(jnp.bfloat16)
        grad_here = grad_mixed[first:last]
        grad_values = grad_values.at[:last].add(
            jnp.einsum("kgqp,qkgd->pkd", attend_low, grad_here, preferred_element_type=jnp.float32)
        )
        grad_attend = jnp.einsum(
            "qkgd,pkd->kgqp", grad_here, values[:last], preferred_element_type=jnp.float32
        )
        inner = jnp.sum(attend * grad_attend, axis=-1, keepdims=True)
        grad_scores = (attend * (grad_attend - inner)).astype(jnp.bfloat16)
        query_parts.append(
            jnp.einsum(
                "kgqp,pkd->qkgd", grad_scores, keys[:last], preferred_element_type=jnp.float32
            )
            * scale
        )
        grad_keys = grad_keys.at[:last].add(
            jnp.einsum(
                "kgqp,qkgd->pkd",
                grad_scores,
                queries[first:last],
                preferred_element_type=jnp.float32,
            )
            * scale
        )
    grad_queries = jnp.concatenate(query_parts, axis=0).reshape(group_rows, heads, head_dim)

    def query_side(values_in, gain_in):
        return rotated(values_in, gain_in, cosine, sine)

    _, query_pull = jax.vjp(query_side, query_pre, query_gain)
    grad_query_pre, grad_query_gain = query_pull(grad_queries)
    _, key_pull = jax.vjp(query_side, key_pre, key_gain)
    grad_key_pre, grad_key_gain = key_pull(grad_keys)
    grad_project = jnp.concatenate(
        [
            grad_query_pre.reshape(group_rows, query_cols),
            grad_key_pre.reshape(group_rows, key_cols),
            grad_values.reshape(group_rows, key_cols),
        ],
        axis=1,
    ).astype(jnp.bfloat16)
    grad_project_w = plane_weight_grad(dot_tl(attn_rows, grad_project).astype(low), 0, plane_bits)
    gain_parts = []

    def grad_rows_part(key):
        part = dot_t(group_slice(grad_project, key), project)
        rows = group_slice(attn_rows, key).astype(jnp.float32)
        gain_parts.append(jnp.sum(part * rows, axis=0))
        return part

    grad_attn_in = sum_to_rows(grad_rows_part)
    grad_attention_gain = sum(gain_parts) / attention_gain
    grad_x_norm, _ = norm_pull(local_x, attention_gain, grad_attn_in)
    grad_tokens = (grad_middle + grad_x_norm).astype(low).reshape(shard_shape)
    gains = jnp.concatenate([grad_attention_gain, grad_feed_gain, grad_query_gain, grad_key_gain])
    for axis, bits in (("tensor", tensor_bits), ("dp", dp_bits)):
        for bit in bits:
            gains = gains + swap(gains, axis, bit)
    sizes = (width, width, head_dim, head_dim)
    gain_outs = []
    at = 0
    for size in sizes:
        gain_outs.append(gains[at : at + size])
        at += size
    return (
        output,
        grad_tokens,
        *gain_outs,
        grad_project_w[:, :query_cols],
        grad_project_w[:, query_cols : query_cols + key_cols],
        grad_project_w[:, query_cols + key_cols :],
        grad_out_w,
        grad_gate_w,
        grad_up_w,
        grad_down_w,
    )


def solution(mesh):
    in_specs = (
        P("dp", None, "tensor", None),
        P("dp", None, "tensor", None),
        P(),
        P(),
        P(),
        P(),
        P(),
        P(),
        P(),
        P("dp", "tensor"),
        P("dp", "tensor"),
        P("dp", "tensor"),
        P("tensor", "dp"),
        P("dp", "tensor"),
        P("dp", "tensor"),
        P("tensor", "dp"),
    )
    out_specs = (
        P("dp", None, "tensor", None),
        P("dp", None, "tensor", None),
        P(),
        P(),
        P(),
        P(),
        P("dp", "tensor"),
        P("dp", "tensor"),
        P("dp", "tensor"),
        P("tensor", "dp"),
        P("dp", "tensor"),
        P("dp", "tensor"),
        P("tensor", "dp"),
    )
    return jax.shard_map(
        on_device, mesh=mesh, in_specs=in_specs, out_specs=out_specs, check_vma=False
    )
```

```python
import jax
import jax.numpy as jnp
from jax import lax
from jax.sharding import PartitionSpec as P

BLOCK = 128
QROWS = 512


EPS = 1e-05
THETA = 1000000.0
NEG = -1e30


def norm_rows(values, gain):
    return values * lax.rsqrt(jnp.mean(values * values, axis=-1, keepdims=True) + EPS) * gain


def norm_pull(values, gain, grad):
    inverse = lax.rsqrt(jnp.mean(values * values, axis=-1, keepdims=True) + EPS)
    scaled = grad * gain
    inner = jnp.mean(values * scaled, axis=-1, keepdims=True)
    grad_values = inverse * scaled - values * (inverse * inverse * inverse * inner)
    return grad_values, jnp.sum(grad * values * inverse, axis=0)


def turn_half(values):
    half = values.shape[-1] // 2
    return jnp.concatenate([-values[..., half:], values[..., :half]], axis=-1)


def rotated(values, gain, cosine, sine):
    normed = norm_rows(values, gain)
    return normed * cosine + turn_half(normed) * sine


def swap(values, axis, bit):
    count = lax.axis_size(axis)
    return lax.ppermute(values, axis, [(index, index ^ bit) for index in range(count)])


def bits_of(count):
    bits = []
    bit = 1
    while bit < count:
        bits.append(bit)
        bit *= 2
    return bits


def dot(left, right):
    return jnp.dot(left, right, preferred_element_type=jnp.float32)


def dot_t(left, right):
    return lax.dot_general(
        left, right, (((1,), (1,)), ((), ())), preferred_element_type=jnp.float32
    )


def dot_tl(left, right):
    return lax.dot_general(
        left, right, (((0,), (0,)), ((), ())), preferred_element_type=jnp.float32
    )


def spread(pieces, axis, bits):
    pieces = dict(pieces)
    for bit in bits:
        for key in sorted(pieces):
            pieces[key | bit] = swap(pieces[key], axis, bit)
    return pieces


def fold(pieces, axis, bits):
    pieces = dict(pieces)
    for bit in bits:
        for key in sorted(pieces, reverse=True):
            if key & bit:
                got = swap(pieces.pop(key).astype(jnp.bfloat16), axis, bit)
                pieces[key ^ bit] = pieces[key ^ bit] + got.astype(jnp.float32)
    return pieces


def widen(values, index, axis, bit, at):
    got = swap(values, axis, bit)
    upper = (index & bit) != 0
    return jnp.stack([jnp.where(upper, got, values), jnp.where(upper, values, got)], axis=at)


def halve(values, index, axis, bit, at):
    mine = ((index & bit) != 0).astype(jnp.int32)
    keep = lax.dynamic_index_in_dim(values, mine, at, keepdims=False)
    send = lax.dynamic_index_in_dim(values, 1 - mine, at, keepdims=False)
    got = swap(send, axis, bit)
    return (keep.astype(jnp.float32) + got.astype(jnp.float32)).astype(jnp.bfloat16)


def place(pieces, index, dim, count):
    first = pieces[0]
    shape = list(first.shape)
    size = shape[dim]
    shape[dim] = size * count
    whole = jnp.zeros(shape, first.dtype)
    for key, block in pieces.items():
        whole = lax.dynamic_update_slice_in_dim(whole, block, (index ^ key) * size, dim)
    return whole


def on_device(
    tokens,
    cotangent,
    lengths,
    groups,
    offsets,
    attention_gain,
    feed_gain,
    query_gain,
    key_gain,
    query_weight,
    key_weight,
    value_weight,
    out_weight,
    gate_weight,
    up_weight,
    down_weight,
):
    shard_shape = tokens.shape
    units, unit, width = shard_shape[1:]
    tensor_count = lax.axis_size("tensor")
    dp_count = lax.axis_size("dp")
    tensor_at = lax.axis_index("tensor")
    group = lax.axis_index("dp")
    first_core = (group & 1) == 0
    far = tensor_count // 2
    local_rows = units * unit
    group_rows = local_rows * tensor_count
    head_dim = query_gain.shape[0]
    tensor_bits = bits_of(tensor_count)
    near_bits = tensor_bits[:-1]
    dp_bits = bits_of(dp_count)
    plane_bits = dp_bits[1:]
    plane_back = plane_bits[::-1]
    low = jnp.bfloat16

    def rows_of_group(block):
        pieces = spread({0: block.reshape(units, unit, width)}, "tensor", tensor_bits[::-1])
        return place(pieces, tensor_at, 1, tensor_count).reshape(group_rows, width)

    def sum_to_rows(make):
        pieces = {key: make(key) for key in range(tensor_count - 1, -1, -1)}
        return fold(pieces, "tensor", tensor_bits)[0]

    def group_slice(whole, key):
        cube = whole.reshape(units, unit * tensor_count, whole.shape[-1])
        part = lax.dynamic_slice_in_dim(cube, (tensor_at ^ key) * unit, unit, 1)
        return part.reshape(local_rows, whole.shape[-1])

    def feed_spread(block):
        pieces = spread({0: block}, "tensor", near_bits[::-1])
        own = jnp.concatenate([pieces[key] for key in sorted(pieces)], axis=0)
        return jnp.concatenate([own, swap(own, "dp", 1)], axis=0)

    def feed_fold(make):
        got = swap(make(1).astype(low), "dp", 1)
        total = make(0) + got.astype(jnp.float32)
        pieces = {
            key: lax.slice_in_dim(total, key * local_rows, (key + 1) * local_rows, axis=0)
            for key in range(far)
        }
        return fold(pieces, "tensor", near_bits)[0]

    def order_at(bit, held):
        return sum(1 for other in held if other > bit)

    def gather_plane(values, held, order):
        held = list(held)
        for bit in order:
            values = widen(values, group, "dp", bit, order_at(bit, held))
            held.append(bit)
        return values

    def scatter_plane(values, held, order):
        held = list(held)
        for bit in order:
            held.remove(bit)
            values = halve(values, group, "dp", bit, order_at(bit, held))
        return values

    def feed_pair(shard):
        other = swap(shard, "tensor", far)
        got = swap(jnp.where(first_core, other, shard), "dp", 1)
        return jnp.stack(
            [jnp.where(first_core, shard, got), jnp.where(first_core, got, other)], axis=0
        )

    def feed_pair_grad(pair):
        mine = (group & 1).astype(jnp.int32)
        keep = lax.dynamic_index_in_dim(pair, mine, 0, keepdims=False)
        got = swap(lax.dynamic_index_in_dim(pair, 1 - mine, 0, keepdims=False), "dp", 1)
        near = jnp.where(first_core, keep, got).astype(jnp.float32)
        return near + swap(jnp.where(first_core, got, keep), "tensor", far).astype(jnp.float32)

    local_x = tokens.reshape(local_rows, width).astype(jnp.float32)
    attn_rows = rows_of_group(norm_rows(local_x, attention_gain).astype(low))
    query_cols = query_weight.shape[1]
    key_cols = key_weight.shape[1]
    heads = query_cols // head_dim
    value_heads = key_cols // head_dim
    repeat = heads // value_heads
    hidden_cols = gate_weight.shape[1]
    shard_rows = query_weight.shape[0]
    half_rows = shard_rows // 2
    attn_pack = gather_plane(
        jnp.concatenate([query_weight, key_weight, value_weight, out_weight.T], axis=1),
        [],
        plane_bits + [1],
    ).reshape(width, query_cols + 2 * key_cols + query_cols)
    project = attn_pack[:, : query_cols + 2 * key_cols]
    out_turned = attn_pack[:, query_cols + 2 * key_cols :]
    down_turned = down_weight.T
    pack_a = gather_plane(
        feed_pair(jnp.concatenate([gate_weight, down_turned[:half_rows]], axis=0)), [1], plane_bits
    ).reshape(dp_count, shard_rows + half_rows, hidden_cols)
    pack_b = gather_plane(
        feed_pair(jnp.concatenate([up_weight, down_turned[half_rows:]], axis=0)), [1], plane_back
    ).reshape(dp_count, shard_rows + half_rows, hidden_cols)
    gate_full = pack_a[:, :shard_rows].reshape(width, hidden_cols)
    up_full = pack_b[:, :shard_rows].reshape(width, hidden_cols)
    down_full = jnp.concatenate([pack_a[:, shard_rows:], pack_b[:, shard_rows:]], axis=1).reshape(
        width, hidden_cols
    )
    local_back = cotangent.reshape(local_rows, width)
    back_rows = feed_spread(local_back)

    position = jnp.arange(group_rows, dtype=jnp.int32)
    start = offsets * BLOCK
    finish = start + lengths
    number = jnp.arange(lengths.shape[0], dtype=jnp.int32)
    inside = (
        (groups[None, :] == group)
        & (position[:, None] >= start[None, :])
        & (position[:, None] < finish[None, :])
    ).astype(jnp.int32)
    segment = jnp.sum(inside * (number + 1)[None, :], axis=1) - 1
    segment = jnp.where(segment >= 0, segment, -1 - position)
    inner_pos = jnp.sum(inside * (position[:, None] - start[None, :]), axis=1)
    freq = THETA ** (-(jnp.arange(head_dim // 2, dtype=jnp.float32) * 2.0) / head_dim)
    angle = inner_pos.astype(jnp.float32)[:, None] * freq[None, :]
    cosine = jnp.concatenate([jnp.cos(angle), jnp.cos(angle)], axis=1)[:, None, :]
    sine = jnp.concatenate([jnp.sin(angle), jnp.sin(angle)], axis=1)[:, None, :]

    projected = dot(attn_rows, project)
    query_pre = projected[:, :query_cols].reshape(group_rows, heads, head_dim)
    key_pre = projected[:, query_cols : query_cols + key_cols].reshape(
        group_rows, value_heads, head_dim
    )
    value_pre = projected[:, query_cols + key_cols :]
    queries = (
        rotated(query_pre, query_gain, cosine, sine)
        .astype(jnp.bfloat16)
        .reshape(group_rows, value_heads, repeat, head_dim)
    )
    keys = rotated(key_pre, key_gain, cosine, sine).astype(jnp.bfloat16)
    values = value_pre.astype(jnp.bfloat16).reshape(group_rows, value_heads, head_dim)
    scale = head_dim ** (-0.5)
    block_count = group_rows // QROWS

    def block_scores(index):
        first = index * QROWS
        last = first + QROWS
        scores = (
            jnp.einsum(
                "qkgd,pkd->kgqp",
                queries[first:last],
                keys[:last],
                preferred_element_type=jnp.float32,
            )
            * scale
        )
        allowed = (segment[first:last, None] == segment[None, :last]) & (
            position[None, :last] <= position[first:last, None]
        )
        return jnp.where(allowed, scores, NEG)

    mixed_parts = []
    log_totals = []
    for index in range(block_count):
        last = (index + 1) * QROWS
        scores = block_scores(index)
        summit = jnp.max(scores, axis=-1, keepdims=True)
        shifted = jnp.exp(scores - summit)
        total = jnp.sum(shifted, axis=-1, keepdims=True)
        attend = (shifted / total).astype(jnp.bfloat16)
        log_totals.append(summit + jnp.log(total))
        mixed_parts.append(
            jnp.einsum("kgqp,pkd->qkgd", attend, values[:last], preferred_element_type=jnp.float32)
        )
    mixed = (
        jnp.concatenate(mixed_parts, axis=0)
        .reshape(group_rows, heads * head_dim)
        .astype(jnp.bfloat16)
    )
    attn_out = sum_to_rows(lambda key: dot_t(group_slice(mixed, key), out_turned))
    middle = local_x + attn_out
    feed_rows = feed_spread(norm_rows(middle, feed_gain).astype(low))
    gate = dot(feed_rows, gate_full)
    up = dot(feed_rows, up_full)
    grad_hidden = dot(back_rows, down_full)
    sigmoid = jax.nn.sigmoid(gate)
    silu = gate * sigmoid
    hidden = (silu * up).astype(low)
    grad_gate = (grad_hidden * up * sigmoid * (1.0 + gate * (1.0 - sigmoid))).astype(low)
    grad_up = (grad_hidden * silu).astype(low)

    half_group = far * local_rows

    def part_of(whole, part):
        return lax.slice_in_dim(whole, part * half_group, (part + 1) * half_group, axis=0)

    grad_feed_in = feed_fold(
        lambda part: dot_t(part_of(grad_gate, part), gate_full)
        + dot_t(part_of(grad_up, part), up_full)
    )
    feed_out = feed_fold(lambda part: dot_t(part_of(hidden, part), down_full))
    output = (middle + feed_out).astype(low).reshape(shard_shape)
    grad_middle_norm, grad_feed_gain = norm_pull(middle, feed_gain, grad_feed_in)
    grad_middle = local_back.astype(jnp.float32) + grad_middle_norm
    back_attn = rows_of_group(grad_middle.astype(low))
    cube = [2] * len(dp_bits)
    by_shard = (dp_count, shard_rows, hidden_cols)
    grad_gate_full = dot_tl(feed_rows, grad_gate).astype(low).reshape(by_shard)
    grad_up_full = dot_tl(feed_rows, grad_up).astype(low).reshape(by_shard)
    grad_down_full = dot_tl(back_rows, hidden).astype(low).reshape(by_shard)

    def feed_grad(main, rest, order):
        packed = jnp.concatenate([main, rest], axis=1).reshape(
            *cube, shard_rows + half_rows, hidden_cols
        )
        return feed_pair_grad(scatter_plane(packed, dp_bits, order))

    part_a = feed_grad(grad_gate_full, grad_down_full[:, :half_rows], plane_bits)
    part_b = feed_grad(grad_up_full, grad_down_full[:, half_rows:], plane_back)
    grad_gate_w = part_a[:shard_rows]
    grad_up_w = part_b[:shard_rows]
    grad_down_w = jnp.concatenate([part_a[shard_rows:], part_b[shard_rows:]], axis=0).T
    grad_out_turned = dot_tl(back_attn, mixed).astype(low)
    grad_mixed = (
        dot(back_attn, out_turned)
        .astype(low)
        .reshape(group_rows, value_heads, repeat, head_dim)
    )
    grad_keys = jnp.zeros((group_rows, value_heads, head_dim), jnp.float32)
    grad_values = jnp.zeros((group_rows, value_heads, head_dim), jnp.float32)
    query_parts = []
    for index in range(block_count):
        first = index * QROWS
        last = first + QROWS
        scores = block_scores(index)
        attend = jnp.exp(scores - log_totals[index])
        attend_low = attend.astype(jnp.bfloat16)
        grad_here = grad_mixed[first:last]
        grad_values = grad_values.at[:last].add(
            jnp.einsum("kgqp,qkgd->pkd", attend_low, grad_here, preferred_element_type=jnp.float32)
        )
        grad_attend = jnp.einsum(
            "qkgd,pkd->kgqp", grad_here, values[:last], preferred_element_type=jnp.float32
        )
        inner = jnp.sum(attend * grad_attend, axis=-1, keepdims=True)
        grad_scores = (attend * (grad_attend - inner)).astype(jnp.bfloat16)
        query_parts.append(
            jnp.einsum(
                "kgqp,pkd->qkgd", grad_scores, keys[:last], preferred_element_type=jnp.float32
            )
            * scale
        )
        grad_keys = grad_keys.at[:last].add(
            jnp.einsum(
                "kgqp,qkgd->pkd",
                grad_scores,
                queries[first:last],
                preferred_element_type=jnp.float32,
            )
            * scale
        )
    grad_queries = jnp.concatenate(query_parts, axis=0).reshape(group_rows, heads, head_dim)

    def query_side(values_in, gain_in):
        return rotated(values_in, gain_in, cosine, sine)

    _, query_pull = jax.vjp(query_side, query_pre, query_gain)
    grad_query_pre, grad_query_gain = query_pull(grad_queries)
    _, key_pull = jax.vjp(query_side, key_pre, key_gain)
    grad_key_pre, grad_key_gain = key_pull(grad_keys)
    grad_project = jnp.concatenate(
        [
            grad_query_pre.reshape(group_rows, query_cols),
            grad_key_pre.reshape(group_rows, key_cols),
            grad_values.reshape(group_rows, key_cols),
        ],
        axis=1,
    ).astype(jnp.bfloat16)
    attn_grad = jnp.concatenate(
        [dot_tl(attn_rows, grad_project).astype(low), grad_out_turned], axis=1
    )
    attn_grad = scatter_plane(
        attn_grad.reshape(*cube, shard_rows, attn_grad.shape[1]), dp_bits, [1] + plane_bits
    ).astype(jnp.float32)
    gain_parts = []

    def grad_rows_part(key):
        part = dot_t(group_slice(grad_project, key), project)
        rows = group_slice(attn_rows, key).astype(jnp.float32)
        gain_parts.append(jnp.sum(part * rows, axis=0))
        return part

    grad_attn_in = sum_to_rows(grad_rows_part)
    grad_attention_gain = sum(gain_parts) / attention_gain
    grad_x_norm, _ = norm_pull(local_x, attention_gain, grad_attn_in)
    grad_tokens = (grad_middle + grad_x_norm).astype(low).reshape(shard_shape)
    gains = jnp.concatenate([grad_attention_gain, grad_feed_gain, grad_query_gain, grad_key_gain])
    for axis, bits in (("tensor", tensor_bits), ("dp", dp_bits)):
        for bit in bits:
            gains = gains + swap(gains, axis, bit)
    sizes = (width, width, head_dim, head_dim)
    gain_outs = []
    at = 0
    for size in sizes:
        gain_outs.append(gains[at : at + size])
        at += size
    return (
        output,
        grad_tokens,
        *gain_outs,
        attn_grad[:, :query_cols],
        attn_grad[:, query_cols : query_cols + key_cols],
        attn_grad[:, query_cols + key_cols : query_cols + 2 * key_cols],
        attn_grad[:, query_cols + 2 * key_cols :].T,
        grad_gate_w,
        grad_up_w,
        grad_down_w,
    )


def solution(mesh):
    in_specs = (
        P("dp", None, "tensor", None),
        P("dp", None, "tensor", None),
        P(),
        P(),
        P(),
        P(),
        P(),
        P(),
        P(),
        P("dp", "tensor"),
        P("dp", "tensor"),
        P("dp", "tensor"),
        P("tensor", "dp"),
        P("dp", "tensor"),
        P("dp", "tensor"),
        P("tensor", "dp"),
    )
    out_specs = (
        P("dp", None, "tensor", None),
        P("dp", None, "tensor", None),
        P(),
        P(),
        P(),
        P(),
        P("dp", "tensor"),
        P("dp", "tensor"),
        P("dp", "tensor"),
        P("tensor", "dp"),
        P("dp", "tensor"),
        P("dp", "tensor"),
        P("tensor", "dp"),
    )
    return jax.shard_map(
        on_device, mesh=mesh, in_specs=in_specs, out_specs=out_specs, check_vma=False
    )
```

```python
import jax
import jax.numpy as jnp
from jax import lax
from jax.sharding import PartitionSpec as P

BLOCK = 128
QROWS = 512


EPS = 1e-05
THETA = 1000000.0
NEG = -1e30


def norm_rows(values, gain):
    return values * lax.rsqrt(jnp.mean(values * values, axis=-1, keepdims=True) + EPS) * gain


def norm_pull(values, gain, grad):
    inverse = lax.rsqrt(jnp.mean(values * values, axis=-1, keepdims=True) + EPS)
    scaled = grad * gain
    inner = jnp.mean(values * scaled, axis=-1, keepdims=True)
    grad_values = inverse * scaled - values * (inverse * inverse * inverse * inner)
    return grad_values, jnp.sum(grad * values * inverse, axis=0)


def turn_half(values):
    half = values.shape[-1] // 2
    return jnp.concatenate([-values[..., half:], values[..., :half]], axis=-1)


def rotated(values, gain, cosine, sine):
    normed = norm_rows(values, gain)
    return normed * cosine + turn_half(normed) * sine


def after(values, *others):
    return lax.optimization_barrier((values, others))[0]


def swap(values, axis, bit):
    count = lax.axis_size(axis)
    return lax.ppermute(values, axis, [(index, index ^ bit) for index in range(count)])


def bits_of(count):
    bits = []
    bit = 1
    while bit < count:
        bits.append(bit)
        bit *= 2
    return bits


def dot(left, right):
    return jnp.dot(left, right, preferred_element_type=jnp.float32)


def dot_t(left, right):
    return lax.dot_general(
        left, right, (((1,), (1,)), ((), ())), preferred_element_type=jnp.float32
    )


def dot_tl(left, right):
    return lax.dot_general(
        left, right, (((0,), (0,)), ((), ())), preferred_element_type=jnp.float32
    )


def spread(pieces, axis, bits):
    pieces = dict(pieces)
    for bit in bits:
        for key in sorted(pieces):
            pieces[key | bit] = swap(pieces[key], axis, bit)
    return pieces


def fold(pieces, axis, bits):
    pieces = dict(pieces)
    for bit in bits:
        for key in sorted(pieces, reverse=True):
            if key & bit:
                got = swap(pieces.pop(key).astype(jnp.bfloat16), axis, bit)
                pieces[key ^ bit] = pieces[key ^ bit] + got.astype(jnp.float32)
    return pieces


def widen(values, index, axis, bit):
    got = swap(values, axis, bit)
    upper = (index & bit) != 0
    return jnp.concatenate(
        [jnp.where(upper, got, values), jnp.where(upper, values, got)], axis=0
    )


def halve(values, index, axis, bit):
    size = values.shape[0] // 2
    mine = ((index & bit) != 0).astype(jnp.int32)
    keep = lax.dynamic_slice_in_dim(values, mine * size, size, 0)
    send = lax.dynamic_slice_in_dim(values, (1 - mine) * size, size, 0)
    got = swap(send, axis, bit)
    return (keep.astype(jnp.float32) + got.astype(jnp.float32)).astype(jnp.bfloat16)


def on_device(
    tokens,
    cotangent,
    lengths,
    groups,
    offsets,
    attention_gain,
    feed_gain,
    query_gain,
    key_gain,
    query_weight,
    key_weight,
    value_weight,
    out_weight,
    gate_weight,
    up_weight,
    down_weight,
):
    shard_shape = tokens.shape
    units, unit, width = shard_shape[1:]
    tensor_count = lax.axis_size("tensor")
    dp_count = lax.axis_size("dp")
    tensor_at = lax.axis_index("tensor")
    group = lax.axis_index("dp")
    far = tensor_count // 2
    local_rows = units * unit
    group_rows = local_rows * tensor_count
    head_dim = query_gain.shape[0]
    tensor_bits = bits_of(tensor_count)
    near_bits = tensor_bits[:-1]
    dp_bits = bits_of(dp_count)
    low = jnp.bfloat16
    query_cols = query_weight.shape[1]
    key_cols = key_weight.shape[1]
    heads = query_cols // head_dim
    value_heads = key_cols // head_dim
    repeat = heads // value_heads
    hidden_cols = gate_weight.shape[1]

    def rows_of_group(block):
        pieces = spread({0: block.reshape(units, 1, unit, width)}, "tensor", tensor_bits[::-1])
        whole = jnp.concatenate([pieces[key] for key in range(tensor_count)], axis=1)
        return whole.reshape(group_rows, width)

    def group_slice(whole, key):
        cols = whole.shape[-1]
        part = whole.reshape(units, tensor_count, unit, cols)[:, key]
        return part.reshape(local_rows, cols)

    def row_blocks(block):
        pieces = spread({0: block}, "tensor", tensor_bits[::-1])
        near = jnp.concatenate([pieces[key] for key in range(far)], axis=0)
        distant = jnp.concatenate([pieces[key] for key in range(far, tensor_count)], axis=0)
        return near, distant

    def block_of(near, distant, key):
        half = near if key < far else distant
        at = (key % far) * local_rows
        return lax.slice_in_dim(half, at, at + local_rows, axis=0)

    def sum_to_rows(make, between):
        distant = {key - far: make(key) for key in range(2 * far - 1, far - 1, -1)}
        distant = fold(distant, "tensor", near_bits)[0]
        pieces = {key: make(key) for key in range(far - 1, -1, -1)}
        send = after(distant.astype(low), *between())
        pieces = {key: after(piece, send) for key, piece in pieces.items()}
        got = swap(send, "tensor", far).astype(jnp.float32)
        return fold(pieces, "tensor", near_bits)[0] + got, send

    def whole_weight(shard):
        return lax.all_gather(shard, "dp", axis=0, tiled=True)

    def weight_grad(whole):
        return lax.psum_scatter(whole.astype(low), "dp", scatter_dimension=0, tiled=True)

    def in_turn(blocks):
        picked = [
            lax.dynamic_index_in_dim(blocks, tensor_at ^ key, 0) for key in range(tensor_count)
        ]
        return jnp.concatenate(picked, axis=0)

    local_x = tokens.reshape(local_rows, width).astype(jnp.float32)
    attn_rows = rows_of_group(norm_rows(local_x, attention_gain).astype(low))
    attn_pack = jnp.concatenate([query_weight, key_weight, value_weight, out_weight.T], axis=1)
    for bit in dp_bits:
        attn_pack = widen(attn_pack, group, "dp", bit)
    project = attn_pack[:, : query_cols + 2 * key_cols]
    out_turned = attn_pack[:, query_cols + 2 * key_cols :]
    feed_pack = whole_weight(jnp.concatenate([gate_weight, up_weight, down_weight.T], axis=1))
    gate_full = feed_pack[:, :hidden_cols]
    up_full = feed_pack[:, hidden_cols : 2 * hidden_cols]
    down_full = feed_pack[:, 2 * hidden_cols :]
    local_back = cotangent.reshape(local_rows, width)
    back_near, back_far = row_blocks(after(local_back, attn_rows))
    back_rows = jnp.concatenate([back_near, back_far], axis=0)

    row = jnp.arange(group_rows, dtype=jnp.int32)
    relative = (row // unit) % tensor_count
    position = row + ((relative ^ tensor_at) - relative) * unit
    start = offsets * BLOCK
    finish = start + lengths
    number = jnp.arange(lengths.shape[0], dtype=jnp.int32)
    inside = (
        (groups[None, :] == group)
        & (position[:, None] >= start[None, :])
        & (position[:, None] < finish[None, :])
    ).astype(jnp.int32)
    segment = jnp.sum(inside * (number + 1)[None, :], axis=1) - 1
    segment = jnp.where(segment >= 0, segment, -1 - position)
    inner_pos = jnp.sum(inside * (position[:, None] - start[None, :]), axis=1)
    freq = THETA ** (-(jnp.arange(head_dim // 2, dtype=jnp.float32) * 2.0) / head_dim)
    angle = inner_pos.astype(jnp.float32)[:, None] * freq[None, :]
    cosine = jnp.concatenate([jnp.cos(angle), jnp.cos(angle)], axis=1)[:, None, :]
    sine = jnp.concatenate([jnp.sin(angle), jnp.sin(angle)], axis=1)[:, None, :]

    projected = dot(attn_rows, project)
    query_pre = projected[:, :query_cols].reshape(group_rows, heads, head_dim)
    key_pre = projected[:, query_cols : query_cols + key_cols].reshape(
        group_rows, value_heads, head_dim
    )
    value_pre = projected[:, query_cols + key_cols :]
    queries = (
        rotated(query_pre, query_gain, cosine, sine)
        .astype(jnp.bfloat16)
        .reshape(group_rows, value_heads, repeat, head_dim)
    )
    keys = rotated(key_pre, key_gain, cosine, sine).astype(jnp.bfloat16)
    values = value_pre.astype(jnp.bfloat16).reshape(group_rows, value_heads, head_dim)
    scale = head_dim ** (-0.5)
    block_count = group_rows // QROWS

    def block_scores(index):
        first = index * QROWS
        last = first + QROWS
        scores = (
            jnp.einsum(
                "qkgd,pkd->kgqp",
                queries[first:last],
                keys[:last],
                preferred_element_type=jnp.float32,
            )
            * scale
        )
        allowed = (segment[first:last, None] == segment[None, :last]) & (
            position[None, :last] <= position[first:last, None]
        )
        return jnp.where(allowed, scores, NEG)

    mixed_parts = []
    log_totals = []
    for index in range(block_count):
        last = (index + 1) * QROWS
        scores = block_scores(index)
        summit = jnp.max(scores, axis=-1, keepdims=True)
        shifted = jnp.exp(scores - summit)
        total = jnp.sum(shifted, axis=-1, keepdims=True)
        attend = (shifted / total).astype(jnp.bfloat16)
        log_totals.append(summit + jnp.log(total))
        mixed_parts.append(
            jnp.einsum("kgqp,pkd->qkgd", attend, values[:last], preferred_element_type=jnp.float32)
        )
    mixed = (
        jnp.concatenate(mixed_parts, axis=0)
        .reshape(group_rows, heads * head_dim)
        .astype(jnp.bfloat16)
    )
    mixed = after(mixed, back_near, back_far)
    attn_out, _ = sum_to_rows(
        lambda key: dot_t(group_slice(mixed, key), out_turned), lambda: ()
    )
    middle = local_x + attn_out
    feed_near, feed_far = row_blocks(norm_rows(middle, feed_gain).astype(low))

    def feed(rows, back):
        gate = dot(rows, gate_full)
        up = dot(rows, up_full)
        grad_hidden = dot(back, down_full)
        sigmoid = jax.nn.sigmoid(gate)
        silu = gate * sigmoid
        hidden = (silu * up).astype(low)
        grad_gate = (grad_hidden * up * sigmoid * (1.0 + gate * (1.0 - sigmoid))).astype(low)
        grad_up = (grad_hidden * silu).astype(low)
        return hidden, grad_gate, grad_up

    near_parts = feed(feed_near, back_near)
    far_parts = feed(after(feed_far, near_parts), back_far)

    def grad_feed_part(key):
        return dot_t(block_of(near_parts[1], far_parts[1], key), gate_full) + dot_t(
            block_of(near_parts[2], far_parts[2], key), up_full
        )

    grad_feed_in, _ = sum_to_rows(grad_feed_part, lambda: ())
    hidden, grad_gate, grad_up = (
        jnp.concatenate([one, two], axis=0) for one, two in zip(near_parts, far_parts)
    )
    feed_rows = jnp.concatenate([feed_near, feed_far], axis=0)
    hidden, grad_gate, grad_up = after((hidden, grad_gate, grad_up), grad_feed_in)
    grad_feed_pack = jnp.concatenate(
        [
            dot_tl(feed_rows, grad_gate).astype(low),
            dot_tl(feed_rows, grad_up).astype(low),
            dot_tl(back_rows, hidden).astype(low),
        ],
        axis=1,
    )
    grad_feed_w = weight_grad(grad_feed_pack).astype(jnp.float32)
    grad_middle_norm, grad_feed_gain = norm_pull(middle, feed_gain, grad_feed_in)
    grad_middle = local_back.astype(jnp.float32) + grad_middle_norm
    back_attn = rows_of_group(grad_middle.astype(low))
    feed_part = in_turn(dot_t(hidden, down_full).astype(low).reshape(tensor_count, local_rows, width))
    back_attn, feed_part = after((back_attn, feed_part), grad_feed_pack)
    feed_out = lax.psum_scatter(feed_part, "tensor", scatter_dimension=0, tiled=True).reshape(
        local_rows, width
    )
    output = (middle + feed_out.astype(jnp.float32)).astype(low).reshape(shard_shape)
    grad_out_turned = dot_tl(back_attn, mixed).astype(low)
    grad_mixed = (
        dot(back_attn, out_turned)
        .astype(low)
        .reshape(group_rows, value_heads, repeat, head_dim)
    )
    grad_keys = jnp.zeros((group_rows, value_heads, head_dim), jnp.float32)
    grad_values = jnp.zeros((group_rows, value_heads, head_dim), jnp.float32)
    query_parts = []
    for index in range(block_count - 1, -1, -1):
        first = index * QROWS
        last = first + QROWS
        scores = block_scores(index)
        attend = jnp.exp(scores - log_totals[index])
        attend_low = attend.astype(jnp.bfloat16)
        grad_here = grad_mixed[first:last]
        grad_values = grad_values.at[:last].add(
            jnp.einsum("kgqp,qkgd->pkd", attend_low, grad_here, preferred_element_type=jnp.float32)
        )
        grad_attend = jnp.einsum(
            "qkgd,pkd->kgqp", grad_here, values[:last], preferred_element_type=jnp.float32
        )
        inner = jnp.sum(attend * grad_attend, axis=-1, keepdims=True)
        grad_scores = (attend * (grad_attend - inner)).astype(jnp.bfloat16)
        query_parts.append(
            jnp.einsum(
                "kgqp,pkd->qkgd", grad_scores, keys[:last], preferred_element_type=jnp.float32
            )
            * scale
        )
        grad_keys = grad_keys.at[:last].add(
            jnp.einsum(
                "kgqp,qkgd->pkd",
                grad_scores,
                queries[first:last],
                preferred_element_type=jnp.float32,
            )
            * scale
        )
    query_parts = query_parts[::-1]
    grad_queries = jnp.concatenate(query_parts, axis=0).reshape(group_rows, heads, head_dim)

    def query_side(values_in, gain_in):
        return rotated(values_in, gain_in, cosine, sine)

    _, query_pull = jax.vjp(query_side, query_pre, query_gain)
    grad_query_pre, grad_query_gain = query_pull(grad_queries)
    _, key_pull = jax.vjp(query_side, key_pre, key_gain)
    grad_key_pre, grad_key_gain = key_pull(grad_keys)
    grad_project = jnp.concatenate(
        [
            grad_query_pre.reshape(group_rows, query_cols),
            grad_key_pre.reshape(group_rows, key_cols),
            grad_values.reshape(group_rows, key_cols),
        ],
        axis=1,
    ).astype(jnp.bfloat16)
    later = {}

    def grad_rows_part(key):
        part = dot_t(group_slice(grad_project, key), project)
        if key == 2 * far - 1:
            later["project"] = after(grad_project, part)
        return part

    def tail_between():
        full = dot_tl(attn_rows, later["project"])
        grad_attention_gain = jnp.sum(full * project.astype(jnp.float32), axis=1) / attention_gain
        pack = jnp.concatenate([full.astype(low), grad_out_turned], axis=1)
        gains = jnp.concatenate(
            [grad_attention_gain, grad_feed_gain, grad_query_gain, grad_key_gain]
        )
        for bit in near_bits:
            gains = gains + swap(gains, "tensor", bit)
        later["gains"] = gains
        later["sums"] = halve(pack, group, "dp", dp_bits[-1])
        return gains, grad_feed_w

    grad_attn_in, attn_sent = sum_to_rows(grad_rows_part, tail_between)
    gains = after(later["gains"], attn_sent)
    gains = gains + swap(gains, "tensor", far)
    for bit in dp_bits[::-1]:
        gains = gains + swap(gains, "dp", bit)
    attn_grad = later["sums"]
    for bit in dp_bits[-2::-1]:
        attn_grad = halve(attn_grad, group, "dp", bit)
    grad_attn_in, attn_grad, gains = lax.optimization_barrier((grad_attn_in, attn_grad, gains))
    grad_x_norm, _ = norm_pull(local_x, attention_gain, grad_attn_in)
    grad_tokens = (grad_middle + grad_x_norm).astype(low).reshape(shard_shape)
    sizes = (width, width, head_dim, head_dim)
    gain_outs = []
    at = 0
    for size in sizes:
        gain_outs.append(gains[at : at + size])
        at += size
    return (
        output,
        grad_tokens,
        *gain_outs,
        attn_grad[:, :query_cols].astype(jnp.float32),
        attn_grad[:, query_cols : query_cols + key_cols].astype(jnp.float32),
        attn_grad[:, query_cols + key_cols : query_cols + 2 * key_cols].astype(jnp.float32),
        attn_grad[:, query_cols + 2 * key_cols :].astype(jnp.float32).T,
        grad_feed_w[:, :hidden_cols],
        grad_feed_w[:, hidden_cols : 2 * hidden_cols],
        grad_feed_w[:, 2 * hidden_cols :].T,
    )


def solution(mesh):
    in_specs = (
        P("dp", None, "tensor", None),
        P("dp", None, "tensor", None),
        P(),
        P(),
        P(),
        P(),
        P(),
        P(),
        P(),
        P("dp", "tensor"),
        P("dp", "tensor"),
        P("dp", "tensor"),
        P("tensor", "dp"),
        P("dp", "tensor"),
        P("dp", "tensor"),
        P("tensor", "dp"),
    )
    out_specs = (
        P("dp", None, "tensor", None),
        P("dp", None, "tensor", None),
        P(),
        P(),
        P(),
        P(),
        P("dp", "tensor"),
        P("dp", "tensor"),
        P("dp", "tensor"),
        P("tensor", "dp"),
        P("dp", "tensor"),
        P("dp", "tensor"),
        P("tensor", "dp"),
    )
    return jax.shard_map(
        on_device, mesh=mesh, in_specs=in_specs, out_specs=out_specs, check_vma=False
    )
```

```python
import jax
import jax.numpy as jnp
from jax import lax
from jax.sharding import PartitionSpec as P

BLOCK = 128
QROWS = 512


EPS = 1e-05
THETA = 1000000.0
NEG = -1e30


def norm_rows(values, gain):
    return values * lax.rsqrt(jnp.mean(values * values, axis=-1, keepdims=True) + EPS) * gain


def norm_pull(values, gain, grad):
    inverse = lax.rsqrt(jnp.mean(values * values, axis=-1, keepdims=True) + EPS)
    scaled = grad * gain
    inner = jnp.mean(values * scaled, axis=-1, keepdims=True)
    grad_values = inverse * scaled - values * (inverse * inverse * inverse * inner)
    return grad_values, jnp.sum(grad * values * inverse, axis=0)


def turn_half(values):
    half = values.shape[-1] // 2
    return jnp.concatenate([-values[..., half:], values[..., :half]], axis=-1)


def rotated(values, gain, cosine, sine):
    normed = norm_rows(values, gain)
    return normed * cosine + turn_half(normed) * sine


def after(values, *others):
    return lax.optimization_barrier((values, others))[0]


def swap(values, axis, bit):
    count = lax.axis_size(axis)
    return lax.ppermute(values, axis, [(index, index ^ bit) for index in range(count)])


def bits_of(count):
    bits = []
    bit = 1
    while bit < count:
        bits.append(bit)
        bit *= 2
    return bits


def dot(left, right):
    return jnp.dot(left, right, preferred_element_type=jnp.float32)


def dot_t(left, right):
    return lax.dot_general(
        left, right, (((1,), (1,)), ((), ())), preferred_element_type=jnp.float32
    )


def dot_tl(left, right):
    return lax.dot_general(
        left, right, (((0,), (0,)), ((), ())), preferred_element_type=jnp.float32
    )


def spread(pieces, axis, bits):
    pieces = dict(pieces)
    for bit in bits:
        for key in sorted(pieces):
            pieces[key | bit] = swap(pieces[key], axis, bit)
    return pieces


def fold(pieces, axis, bits, arrived=None):
    pieces = dict(pieces)
    for bit in bits:
        for key in sorted(pieces, reverse=True):
            if key & bit:
                got = swap(pieces.pop(key).astype(jnp.bfloat16), axis, bit)
                if arrived is not None:
                    arrived.append(got)
                pieces[key ^ bit] = pieces[key ^ bit] + got.astype(jnp.float32)
    return pieces


def widen(values, index, axis, bit, at):
    got = swap(values, axis, bit)
    upper = (index & bit) != 0
    return jnp.stack([jnp.where(upper, got, values), jnp.where(upper, values, got)], axis=at)


def halve(values, index, axis, bit):
    size = values.shape[0] // 2
    mine = ((index & bit) != 0).astype(jnp.int32)
    keep = lax.dynamic_slice_in_dim(values, mine * size, size, 0)
    send = lax.dynamic_slice_in_dim(values, (1 - mine) * size, size, 0)
    got = swap(send, axis, bit)
    return (keep.astype(jnp.float32) + got.astype(jnp.float32)).astype(jnp.bfloat16)


def on_device(
    tokens,
    cotangent,
    lengths,
    groups,
    offsets,
    attention_gain,
    feed_gain,
    query_gain,
    key_gain,
    query_weight,
    key_weight,
    value_weight,
    out_weight,
    gate_weight,
    up_weight,
    down_weight,
):
    shard_shape = tokens.shape
    units, unit, width = shard_shape[1:]
    tensor_count = lax.axis_size("tensor")
    dp_count = lax.axis_size("dp")
    tensor_at = lax.axis_index("tensor")
    group = lax.axis_index("dp")
    far = tensor_count // 2
    local_rows = units * unit
    group_rows = local_rows * tensor_count
    head_dim = query_gain.shape[0]
    tensor_bits = bits_of(tensor_count)
    near_bits = tensor_bits[:-1]
    dp_bits = bits_of(dp_count)
    low = jnp.bfloat16
    query_cols = query_weight.shape[1]
    key_cols = key_weight.shape[1]
    heads = query_cols // head_dim
    value_heads = key_cols // head_dim
    repeat = heads // value_heads
    hidden_cols = gate_weight.shape[1]

    def rows_of_group(block):
        pieces = spread({0: block.reshape(units, 1, unit, width)}, "tensor", tensor_bits[::-1])
        whole = jnp.concatenate([pieces[key] for key in range(tensor_count)], axis=1)
        return whole.reshape(group_rows, width)

    def group_slice(whole, key):
        cols = whole.shape[-1]
        part = whole.reshape(units, tensor_count, unit, cols)[:, key]
        return part.reshape(local_rows, cols)

    def row_blocks(block):
        pieces = spread({0: block}, "tensor", tensor_bits[::-1])
        near = jnp.concatenate([pieces[key] for key in range(far)], axis=0)
        distant = jnp.concatenate([pieces[key] for key in range(far, tensor_count)], axis=0)
        return near, distant

    def block_of(near, distant, key):
        half = near if key < far else distant
        at = (key % far) * local_rows
        return lax.slice_in_dim(half, at, at + local_rows, axis=0)

    def sum_to_rows(make, between):
        distant = {key - far: make(key) for key in range(2 * far - 1, far - 1, -1)}
        distant = fold(distant, "tensor", near_bits)[0]
        pieces = {key: make(key) for key in range(far - 1, -1, -1)}
        send = after(distant.astype(low), *between())
        pieces = {key: after(piece, send) for key, piece in pieces.items()}
        got = swap(send, "tensor", far).astype(jnp.float32)
        arrived = []
        near = fold(pieces, "tensor", near_bits, arrived)[0]
        return near + got, arrived

    def whole_weight(shard):
        return lax.all_gather(shard, "dp", axis=0, tiled=True)

    def weight_grad(whole):
        return lax.psum_scatter(whole.astype(low), "dp", scatter_dimension=0, tiled=True)

    local_x = tokens.reshape(local_rows, width).astype(jnp.float32)
    attn_rows = rows_of_group(norm_rows(local_x, attention_gain).astype(low))
    attn_pack = jnp.concatenate([query_weight, key_weight, value_weight, out_weight.T], axis=1)
    attn_cols = attn_pack.shape[1]
    for bit in dp_bits[1:]:
        attn_pack = widen(attn_pack, group, "dp", bit, 0)
    attn_pack = widen(attn_pack, group, "dp", 1, attn_pack.ndim - 2).reshape(width, attn_cols)
    project = attn_pack[:, : query_cols + 2 * key_cols]
    out_turned = attn_pack[:, query_cols + 2 * key_cols :]
    feed_pack = whole_weight(jnp.concatenate([gate_weight, up_weight, down_weight.T], axis=1))
    gate_full = feed_pack[:, :hidden_cols]
    up_full = feed_pack[:, hidden_cols : 2 * hidden_cols]
    down_full = feed_pack[:, 2 * hidden_cols :]
    local_back = cotangent.reshape(local_rows, width)
    back_near, back_far = row_blocks(after(local_back, attn_rows))
    back_rows = jnp.concatenate([back_near, back_far], axis=0)

    row = jnp.arange(group_rows, dtype=jnp.int32)
    relative = (row // unit) % tensor_count
    position = row + ((relative ^ tensor_at) - relative) * unit
    start = offsets * BLOCK
    finish = start + lengths
    number = jnp.arange(lengths.shape[0], dtype=jnp.int32)
    inside = (
        (groups[None, :] == group)
        & (position[:, None] >= start[None, :])
        & (position[:, None] < finish[None, :])
    ).astype(jnp.int32)
    segment = jnp.sum(inside * (number + 1)[None, :], axis=1) - 1
    segment = jnp.where(segment >= 0, segment, -1 - position)
    inner_pos = jnp.sum(inside * (position[:, None] - start[None, :]), axis=1)
    freq = THETA ** (-(jnp.arange(head_dim // 2, dtype=jnp.float32) * 2.0) / head_dim)
    angle = inner_pos.astype(jnp.float32)[:, None] * freq[None, :]
    cosine = jnp.concatenate([jnp.cos(angle), jnp.cos(angle)], axis=1)[:, None, :]
    sine = jnp.concatenate([jnp.sin(angle), jnp.sin(angle)], axis=1)[:, None, :]

    projected = dot(attn_rows, project)
    query_pre = projected[:, :query_cols].reshape(group_rows, heads, head_dim)
    key_pre = projected[:, query_cols : query_cols + key_cols].reshape(
        group_rows, value_heads, head_dim
    )
    value_pre = projected[:, query_cols + key_cols :]
    queries = (
        rotated(query_pre, query_gain, cosine, sine)
        .astype(jnp.bfloat16)
        .reshape(group_rows, value_heads, repeat, head_dim)
    )
    keys = rotated(key_pre, key_gain, cosine, sine).astype(jnp.bfloat16)
    values = value_pre.astype(jnp.bfloat16).reshape(group_rows, value_heads, head_dim)
    scale = head_dim ** (-0.5)
    block_count = group_rows // QROWS

    def block_scores(index):
        first = index * QROWS
        last = first + QROWS
        scores = (
            jnp.einsum(
                "qkgd,pkd->kgqp",
                queries[first:last],
                keys[:last],
                preferred_element_type=jnp.float32,
            )
            * scale
        )
        allowed = (segment[first:last, None] == segment[None, :last]) & (
            position[None, :last] <= position[first:last, None]
        )
        return jnp.where(allowed, scores, NEG)

    mixed_parts = []
    log_totals = []
    for index in range(block_count):
        last = (index + 1) * QROWS
        scores = block_scores(index)
        summit = jnp.max(scores, axis=-1, keepdims=True)
        shifted = jnp.exp(scores - summit)
        total = jnp.sum(shifted, axis=-1, keepdims=True)
        attend = (shifted / total).astype(jnp.bfloat16)
        log_totals.append(summit + jnp.log(total))
        mixed_parts.append(
            jnp.einsum("kgqp,pkd->qkgd", attend, values[:last], preferred_element_type=jnp.float32)
        )
    mixed = (
        jnp.concatenate(mixed_parts, axis=0)
        .reshape(group_rows, heads * head_dim)
        .astype(jnp.bfloat16)
    )
    mixed = after(mixed, back_near, back_far)
    attn_out, _ = sum_to_rows(
        lambda key: dot_t(group_slice(mixed, key), out_turned), lambda: ()
    )
    attn_out = after(attn_out, feed_pack)
    middle = local_x + attn_out
    feed_near, feed_far = row_blocks(norm_rows(middle, feed_gain).astype(low))

    def feed(rows, back):
        gate = dot(rows, gate_full)
        up = dot(rows, up_full)
        grad_hidden = dot(back, down_full)
        sigmoid = jax.nn.sigmoid(gate)
        silu = gate * sigmoid
        hidden = (silu * up).astype(low)
        grad_gate = (grad_hidden * up * sigmoid * (1.0 + gate * (1.0 - sigmoid))).astype(low)
        grad_up = (grad_hidden * silu).astype(low)
        return hidden, grad_gate, grad_up

    near_parts = feed(feed_near, back_near)
    far_parts = feed(after(feed_far, near_parts), back_far)

    def grad_feed_part(key):
        return dot_t(block_of(near_parts[1], far_parts[1], key), gate_full) + dot_t(
            block_of(near_parts[2], far_parts[2], key), up_full
        )

    grad_feed_in, _ = sum_to_rows(grad_feed_part, lambda: ())
    hidden, grad_gate, grad_up = (
        jnp.concatenate([one, two], axis=0) for one, two in zip(near_parts, far_parts)
    )
    feed_rows = jnp.concatenate([feed_near, feed_far], axis=0)
    hidden, grad_gate, grad_up = after((hidden, grad_gate, grad_up), grad_feed_in)
    grad_feed_pack = jnp.concatenate(
        [
            dot_tl(feed_rows, grad_gate).astype(low),
            dot_tl(feed_rows, grad_up).astype(low),
            dot_tl(back_rows, hidden).astype(low),
        ],
        axis=1,
    )
    grad_feed_w = weight_grad(grad_feed_pack).astype(jnp.float32)
    grad_middle_norm, grad_feed_gain = norm_pull(middle, feed_gain, grad_feed_in)
    grad_middle = local_back.astype(jnp.float32) + grad_middle_norm
    back_attn = rows_of_group(grad_middle.astype(low))
    back_attn = after(back_attn, grad_feed_pack)
    grad_out_turned = dot_tl(back_attn, mixed).astype(low)
    grad_mixed = (
        dot(back_attn, out_turned)
        .astype(low)
        .reshape(group_rows, value_heads, repeat, head_dim)
    )
    grad_keys = jnp.zeros((group_rows, value_heads, head_dim), jnp.float32)
    grad_values = jnp.zeros((group_rows, value_heads, head_dim), jnp.float32)
    query_parts = []
    for index in range(block_count - 1, -1, -1):
        first = index * QROWS
        last = first + QROWS
        scores = block_scores(index)
        attend = jnp.exp(scores - log_totals[index])
        attend_low = attend.astype(jnp.bfloat16)
        grad_here = grad_mixed[first:last]
        grad_values = grad_values.at[:last].add(
            jnp.einsum("kgqp,qkgd->pkd", attend_low, grad_here, preferred_element_type=jnp.float32)
        )
        grad_attend = jnp.einsum(
            "qkgd,pkd->kgqp", grad_here, values[:last], preferred_element_type=jnp.float32
        )
        inner = jnp.sum(attend * grad_attend, axis=-1, keepdims=True)
        grad_scores = (attend * (grad_attend - inner)).astype(jnp.bfloat16)
        if index == block_count - 1:
            first_block = grad_scores
        query_parts.append(
            jnp.einsum(
                "kgqp,pkd->qkgd", grad_scores, keys[:last], preferred_element_type=jnp.float32
            )
            * scale
        )
        grad_keys = grad_keys.at[:last].add(
            jnp.einsum(
                "kgqp,qkgd->pkd",
                grad_scores,
                queries[first:last],
                preferred_element_type=jnp.float32,
            )
            * scale
        )
    query_parts = query_parts[::-1]
    feed_out, _ = sum_to_rows(
        lambda key: dot_t(
            lax.slice_in_dim(hidden, key * local_rows, (key + 1) * local_rows, axis=0), down_full
        ),
        lambda: (first_block,),
    )
    output = (middle + feed_out).astype(low).reshape(shard_shape)
    grad_queries = jnp.concatenate(query_parts, axis=0).reshape(group_rows, heads, head_dim)

    def query_side(values_in, gain_in):
        return rotated(values_in, gain_in, cosine, sine)

    _, query_pull = jax.vjp(query_side, query_pre, query_gain)
    grad_query_pre, grad_query_gain = query_pull(grad_queries)
    _, key_pull = jax.vjp(query_side, key_pre, key_gain)
    grad_key_pre, grad_key_gain = key_pull(grad_keys)
    grad_project = jnp.concatenate(
        [
            grad_query_pre.reshape(group_rows, query_cols),
            grad_key_pre.reshape(group_rows, key_cols),
            grad_values.reshape(group_rows, key_cols),
        ],
        axis=1,
    ).astype(jnp.bfloat16)
    grad_project = after(grad_project, output)
    later = {}

    def grad_rows_part(key):
        part = dot_t(group_slice(grad_project, key), project)
        if key == 2 * far - 1:
            later["project"] = after(grad_project, part)
        return part

    def tail_between():
        full = dot_tl(attn_rows, later["project"])
        grad_attention_gain = jnp.sum(full * project.astype(jnp.float32), axis=1) / attention_gain
        pack = jnp.concatenate([full.astype(low), grad_out_turned], axis=1)
        gains = jnp.concatenate(
            [grad_attention_gain, grad_feed_gain, grad_query_gain, grad_key_gain]
        )
        later["gains"] = gains
        later["sums"] = halve(pack, group, "dp", dp_bits[-1])
        return (grad_feed_w,)

    grad_attn_in, arrived = sum_to_rows(grad_rows_part, tail_between)
    gains, attn_grad = after((later["gains"], later["sums"]), arrived)
    for bit in tensor_bits:
        gains = gains + swap(gains, "tensor", bit)
    for bit in dp_bits[::-1]:
        gains = gains + swap(gains, "dp", bit)
    for bit in dp_bits[-2::-1]:
        attn_grad = halve(attn_grad, group, "dp", bit)
    grad_x_norm, _ = norm_pull(local_x, attention_gain, grad_attn_in)
    grad_tokens = (grad_middle + grad_x_norm).astype(low).reshape(shard_shape)
    sizes = (width, width, head_dim, head_dim)
    gain_outs = []
    at = 0
    for size in sizes:
        gain_outs.append(gains[at : at + size])
        at += size
    return (
        output,
        grad_tokens,
        *gain_outs,
        attn_grad[:, :query_cols].astype(jnp.float32),
        attn_grad[:, query_cols : query_cols + key_cols].astype(jnp.float32),
        attn_grad[:, query_cols + key_cols : query_cols + 2 * key_cols].astype(jnp.float32),
        attn_grad[:, query_cols + 2 * key_cols :].astype(jnp.float32).T,
        grad_feed_w[:, :hidden_cols],
        grad_feed_w[:, hidden_cols : 2 * hidden_cols],
        grad_feed_w[:, 2 * hidden_cols :].T,
    )


def solution(mesh):
    in_specs = (
        P("dp", None, "tensor", None),
        P("dp", None, "tensor", None),
        P(),
        P(),
        P(),
        P(),
        P(),
        P(),
        P(),
        P("dp", "tensor"),
        P("dp", "tensor"),
        P("dp", "tensor"),
        P("tensor", "dp"),
        P("dp", "tensor"),
        P("dp", "tensor"),
        P("tensor", "dp"),
    )
    out_specs = (
        P("dp", None, "tensor", None),
        P("dp", None, "tensor", None),
        P(),
        P(),
        P(),
        P(),
        P("dp", "tensor"),
        P("dp", "tensor"),
        P("dp", "tensor"),
        P("tensor", "dp"),
        P("dp", "tensor"),
        P("dp", "tensor"),
        P("tensor", "dp"),
    )
    return jax.shard_map(
        on_device, mesh=mesh, in_specs=in_specs, out_specs=out_specs, check_vma=False
    )
```

```python
import jax
import jax.numpy as jnp
from jax import lax
from jax.sharding import PartitionSpec as P

BLOCK = 128
QROWS = 512


EPS = 1e-05
THETA = 1000000.0
NEG = -1e30


def norm_rows(values, gain):
    return values * lax.rsqrt(jnp.mean(values * values, axis=-1, keepdims=True) + EPS) * gain


def norm_pull(values, gain, grad):
    inverse = lax.rsqrt(jnp.mean(values * values, axis=-1, keepdims=True) + EPS)
    scaled = grad * gain
    inner = jnp.mean(values * scaled, axis=-1, keepdims=True)
    grad_values = inverse * scaled - values * (inverse * inverse * inverse * inner)
    return grad_values, jnp.sum(grad * values * inverse, axis=0)


def turn_half(values):
    half = values.shape[-1] // 2
    return jnp.concatenate([-values[..., half:], values[..., :half]], axis=-1)


def rotated(values, gain, cosine, sine):
    normed = norm_rows(values, gain)
    return normed * cosine + turn_half(normed) * sine


def after(values, *others):
    return lax.optimization_barrier((values, others))[0]


def swap(values, axis, bit):
    count = lax.axis_size(axis)
    return lax.ppermute(values, axis, [(index, index ^ bit) for index in range(count)])


def bits_of(count):
    bits = []
    bit = 1
    while bit < count:
        bits.append(bit)
        bit *= 2
    return bits


def dot(left, right):
    return jnp.dot(left, right, preferred_element_type=jnp.float32)


def dot_t(left, right):
    return lax.dot_general(
        left, right, (((1,), (1,)), ((), ())), preferred_element_type=jnp.float32
    )


def dot_tl(left, right):
    return lax.dot_general(
        left, right, (((0,), (0,)), ((), ())), preferred_element_type=jnp.float32
    )


def spread(pieces, axis, bits):
    pieces = dict(pieces)
    for bit in bits:
        for key in sorted(pieces):
            pieces[key | bit] = swap(pieces[key], axis, bit)
    return pieces


def fold(pieces, axis, bits, arrived=None):
    pieces = dict(pieces)
    for bit in bits:
        for key in sorted(pieces, reverse=True):
            if key & bit:
                got = swap(pieces.pop(key).astype(jnp.bfloat16), axis, bit)
                if arrived is not None:
                    arrived.append(got)
                pieces[key ^ bit] = pieces[key ^ bit] + got.astype(jnp.float32)
    return pieces


def widen(values, index, axis, bit, at):
    got = swap(values, axis, bit)
    upper = (index & bit) != 0
    return jnp.stack([jnp.where(upper, got, values), jnp.where(upper, values, got)], axis=at)


def halve(values, index, axis, bit):
    size = values.shape[0] // 2
    mine = ((index & bit) != 0).astype(jnp.int32)
    keep = lax.dynamic_slice_in_dim(values, mine * size, size, 0)
    send = lax.dynamic_slice_in_dim(values, (1 - mine) * size, size, 0)
    got = swap(send, axis, bit)
    return (keep.astype(jnp.float32) + got.astype(jnp.float32)).astype(jnp.bfloat16)


def on_device(
    tokens,
    cotangent,
    lengths,
    groups,
    offsets,
    attention_gain,
    feed_gain,
    query_gain,
    key_gain,
    query_weight,
    key_weight,
    value_weight,
    out_weight,
    gate_weight,
    up_weight,
    down_weight,
):
    shard_shape = tokens.shape
    units, unit, width = shard_shape[1:]
    tensor_count = lax.axis_size("tensor")
    dp_count = lax.axis_size("dp")
    tensor_at = lax.axis_index("tensor")
    group = lax.axis_index("dp")
    far = tensor_count // 2
    local_rows = units * unit
    group_rows = local_rows * tensor_count
    head_dim = query_gain.shape[0]
    tensor_bits = bits_of(tensor_count)
    near_bits = tensor_bits[:-1]
    dp_bits = bits_of(dp_count)
    low = jnp.bfloat16
    query_cols = query_weight.shape[1]
    key_cols = key_weight.shape[1]
    heads = query_cols // head_dim
    value_heads = key_cols // head_dim
    repeat = heads // value_heads
    hidden_cols = gate_weight.shape[1]

    def rows_of_group(block):
        pieces = spread({0: block.reshape(units, 1, unit, width)}, "tensor", tensor_bits[::-1])
        whole = jnp.concatenate([pieces[key] for key in range(tensor_count)], axis=1)
        return whole.reshape(group_rows, width)

    def group_slice(whole, key):
        cols = whole.shape[-1]
        part = whole.reshape(units, tensor_count, unit, cols)[:, key]
        return part.reshape(local_rows, cols)

    def row_blocks(block):
        pieces = spread({0: block}, "tensor", tensor_bits[::-1])
        near = jnp.concatenate([pieces[key] for key in range(far)], axis=0)
        distant = jnp.concatenate([pieces[key] for key in range(far, tensor_count)], axis=0)
        return near, distant

    def block_of(near, distant, key):
        half = near if key < far else distant
        at = (key % far) * local_rows
        return lax.slice_in_dim(half, at, at + local_rows, axis=0)

    def sum_to_rows(make, between):
        distant = {key - far: make(key) for key in range(2 * far - 1, far - 1, -1)}
        distant = fold(distant, "tensor", near_bits)[0]
        pieces = {key: make(key) for key in range(far - 1, -1, -1)}
        send = after(distant.astype(low), *between())
        pieces = {key: after(piece, send) for key, piece in pieces.items()}
        got = swap(send, "tensor", far).astype(jnp.float32)
        arrived = []
        near = fold(pieces, "tensor", near_bits, arrived)[0]
        return near + got, arrived, send

    def whole_weight(shard):
        return lax.all_gather(shard, "dp", axis=0, tiled=True)

    def weight_grad(whole):
        return lax.psum_scatter(whole.astype(low), "dp", scatter_dimension=0, tiled=True)

    local_x = tokens.reshape(local_rows, width).astype(jnp.float32)
    attn_rows = rows_of_group(norm_rows(local_x, attention_gain).astype(low))
    attn_pack = jnp.concatenate([query_weight, key_weight, value_weight, out_weight.T], axis=1)
    attn_cols = attn_pack.shape[1]
    for bit in dp_bits[1:]:
        attn_pack = widen(attn_pack, group, "dp", bit, 0)
    attn_pack = widen(attn_pack, group, "dp", 1, attn_pack.ndim - 2).reshape(width, attn_cols)
    project = attn_pack[:, : query_cols + 2 * key_cols]
    out_turned = attn_pack[:, query_cols + 2 * key_cols :]
    feed_pack = whole_weight(jnp.concatenate([gate_weight, up_weight, down_weight.T], axis=1))
    gate_full = feed_pack[:, :hidden_cols]
    up_full = feed_pack[:, hidden_cols : 2 * hidden_cols]
    down_full = feed_pack[:, 2 * hidden_cols :]
    local_back = cotangent.reshape(local_rows, width)
    back_near, back_far = row_blocks(after(local_back, attn_rows))
    back_rows = jnp.concatenate([back_near, back_far], axis=0)

    row = jnp.arange(group_rows, dtype=jnp.int32)
    relative = (row // unit) % tensor_count
    position = row + ((relative ^ tensor_at) - relative) * unit
    start = offsets * BLOCK
    finish = start + lengths
    number = jnp.arange(lengths.shape[0], dtype=jnp.int32)
    inside = (
        (groups[None, :] == group)
        & (position[:, None] >= start[None, :])
        & (position[:, None] < finish[None, :])
    ).astype(jnp.int32)
    segment = jnp.sum(inside * (number + 1)[None, :], axis=1) - 1
    segment = jnp.where(segment >= 0, segment, -1 - position)
    inner_pos = jnp.sum(inside * (position[:, None] - start[None, :]), axis=1)
    freq = THETA ** (-(jnp.arange(head_dim // 2, dtype=jnp.float32) * 2.0) / head_dim)
    angle = inner_pos.astype(jnp.float32)[:, None] * freq[None, :]
    cosine = jnp.concatenate([jnp.cos(angle), jnp.cos(angle)], axis=1)[:, None, :]
    sine = jnp.concatenate([jnp.sin(angle), jnp.sin(angle)], axis=1)[:, None, :]

    projected = dot(attn_rows, project)
    query_pre = projected[:, :query_cols].reshape(group_rows, heads, head_dim)
    key_pre = projected[:, query_cols : query_cols + key_cols].reshape(
        group_rows, value_heads, head_dim
    )
    value_pre = projected[:, query_cols + key_cols :]
    queries = (
        rotated(query_pre, query_gain, cosine, sine)
        .astype(jnp.bfloat16)
        .reshape(group_rows, value_heads, repeat, head_dim)
    )
    keys = rotated(key_pre, key_gain, cosine, sine).astype(jnp.bfloat16)
    values = value_pre.astype(jnp.bfloat16).reshape(group_rows, value_heads, head_dim)
    scale = head_dim ** (-0.5)
    block_count = group_rows // QROWS

    def block_scores(index):
        first = index * QROWS
        last = first + QROWS
        scores = (
            jnp.einsum(
                "qkgd,pkd->kgqp",
                queries[first:last],
                keys[:last],
                preferred_element_type=jnp.float32,
            )
            * scale
        )
        allowed = (segment[first:last, None] == segment[None, :last]) & (
            position[None, :last] <= position[first:last, None]
        )
        return jnp.where(allowed, scores, NEG)

    mixed_parts = []
    log_totals = []
    for index in range(block_count):
        last = (index + 1) * QROWS
        scores = block_scores(index)
        summit = jnp.max(scores, axis=-1, keepdims=True)
        shifted = jnp.exp(scores - summit)
        total = jnp.sum(shifted, axis=-1, keepdims=True)
        attend = (shifted / total).astype(jnp.bfloat16)
        log_totals.append(summit + jnp.log(total))
        mixed_parts.append(
            jnp.einsum("kgqp,pkd->qkgd", attend, values[:last], preferred_element_type=jnp.float32)
        )
    mixed = (
        jnp.concatenate(mixed_parts, axis=0)
        .reshape(group_rows, heads * head_dim)
        .astype(jnp.bfloat16)
    )
    mixed = after(mixed, back_near, back_far)
    attn_out, _, _ = sum_to_rows(
        lambda key: dot_t(group_slice(mixed, key), out_turned), lambda: ()
    )
    attn_out = after(attn_out, feed_pack)
    middle = local_x + attn_out
    feed_near, feed_far = row_blocks(norm_rows(middle, feed_gain).astype(low))

    def feed(rows, back):
        gate = dot(rows, gate_full)
        up = dot(rows, up_full)
        grad_hidden = dot(back, down_full)
        sigmoid = jax.nn.sigmoid(gate)
        silu = gate * sigmoid
        hidden = (silu * up).astype(low)
        grad_gate = (grad_hidden * up * sigmoid * (1.0 + gate * (1.0 - sigmoid))).astype(low)
        grad_up = (grad_hidden * silu).astype(low)
        return hidden, grad_gate, grad_up

    near_parts = feed(feed_near, back_near)
    far_parts = feed(after(feed_far, near_parts), back_far)

    def grad_feed_part(key):
        return dot_t(block_of(near_parts[1], far_parts[1], key), gate_full) + dot_t(
            block_of(near_parts[2], far_parts[2], key), up_full
        )

    grad_feed_in, _, _ = sum_to_rows(grad_feed_part, lambda: ())
    hidden, grad_gate, grad_up = (
        jnp.concatenate([one, two], axis=0) for one, two in zip(near_parts, far_parts)
    )
    feed_rows = jnp.concatenate([feed_near, feed_far], axis=0)
    hidden, grad_gate, grad_up = after((hidden, grad_gate, grad_up), grad_feed_in)
    grad_feed_pack = jnp.concatenate(
        [
            dot_tl(feed_rows, grad_gate).astype(low),
            dot_tl(feed_rows, grad_up).astype(low),
            dot_tl(back_rows, hidden).astype(low),
        ],
        axis=1,
    )
    grad_feed_w = weight_grad(grad_feed_pack).astype(jnp.float32)
    grad_middle_norm, grad_feed_gain = norm_pull(middle, feed_gain, grad_feed_in)
    grad_middle = local_back.astype(jnp.float32) + grad_middle_norm
    back_attn = rows_of_group(grad_middle.astype(low))
    back_attn = after(back_attn, grad_feed_pack)
    grad_out_turned = dot_tl(back_attn, mixed).astype(low)
    grad_mixed = (
        dot(back_attn, out_turned)
        .astype(low)
        .reshape(group_rows, value_heads, repeat, head_dim)
    )
    grad_keys = jnp.zeros((group_rows, value_heads, head_dim), jnp.float32)
    grad_values = jnp.zeros((group_rows, value_heads, head_dim), jnp.float32)
    query_parts = []
    for index in range(block_count - 1, -1, -1):
        first = index * QROWS
        last = first + QROWS
        scores = block_scores(index)
        attend = jnp.exp(scores - log_totals[index])
        attend_low = attend.astype(jnp.bfloat16)
        grad_here = grad_mixed[first:last]
        grad_values = grad_values.at[:last].add(
            jnp.einsum("kgqp,qkgd->pkd", attend_low, grad_here, preferred_element_type=jnp.float32)
        )
        grad_attend = jnp.einsum(
            "qkgd,pkd->kgqp", grad_here, values[:last], preferred_element_type=jnp.float32
        )
        inner = jnp.sum(attend * grad_attend, axis=-1, keepdims=True)
        grad_scores = (attend * (grad_attend - inner)).astype(jnp.bfloat16)
        if index == block_count - 1:
            first_block = grad_scores
        query_parts.append(
            jnp.einsum(
                "kgqp,pkd->qkgd", grad_scores, keys[:last], preferred_element_type=jnp.float32
            )
            * scale
        )
        grad_keys = grad_keys.at[:last].add(
            jnp.einsum(
                "kgqp,qkgd->pkd",
                grad_scores,
                queries[first:last],
                preferred_element_type=jnp.float32,
            )
            * scale
        )
    query_parts = query_parts[::-1]
    feed_out, feed_arrived, feed_sent = sum_to_rows(
        lambda key: dot_t(
            lax.slice_in_dim(hidden, key * local_rows, (key + 1) * local_rows, axis=0), down_full
        ),
        lambda: (first_block,),
    )
    output = (middle + feed_out).astype(low).reshape(shard_shape)
    grad_queries = jnp.concatenate(query_parts, axis=0).reshape(group_rows, heads, head_dim)

    def query_side(values_in, gain_in):
        return rotated(values_in, gain_in, cosine, sine)

    _, query_pull = jax.vjp(query_side, query_pre, query_gain)
    grad_query_pre, grad_query_gain = query_pull(grad_queries)
    _, key_pull = jax.vjp(query_side, key_pre, key_gain)
    grad_key_pre, grad_key_gain = key_pull(grad_keys)
    grad_project = jnp.concatenate(
        [
            grad_query_pre.reshape(group_rows, query_cols),
            grad_key_pre.reshape(group_rows, key_cols),
            grad_values.reshape(group_rows, key_cols),
        ],
        axis=1,
    ).astype(jnp.bfloat16)
    grad_project = after(grad_project, feed_arrived)
    later = {}

    def grad_rows_part(key):
        part = dot_t(group_slice(grad_project, key), project)
        if key == 2 * far - 1:
            later["project"] = after(grad_project, part)
        return part

    def tail_between():
        full = dot_tl(attn_rows, later["project"])
        grad_attention_gain = jnp.sum(full * project.astype(jnp.float32), axis=1) / attention_gain
        pack = jnp.concatenate([full.astype(low), grad_out_turned], axis=1)
        gains = jnp.concatenate(
            [grad_attention_gain, grad_feed_gain, grad_query_gain, grad_key_gain]
        )
        later["gains"] = gains
        later["sums"] = halve(pack, group, "dp", dp_bits[-1])
        return grad_feed_w, output

    grad_attn_in, arrived, _ = sum_to_rows(grad_rows_part, tail_between)
    gains, attn_grad = after((later["gains"], later["sums"]), arrived)
    for bit in tensor_bits:
        gains = gains + swap(gains, "tensor", bit)
    for bit in dp_bits[::-1]:
        gains = gains + swap(gains, "dp", bit)
    for bit in dp_bits[-2::-1]:
        attn_grad = halve(attn_grad, group, "dp", bit)
    grad_x_norm, _ = norm_pull(local_x, attention_gain, grad_attn_in)
    grad_tokens = (grad_middle + grad_x_norm).astype(low).reshape(shard_shape)
    sizes = (width, width, head_dim, head_dim)
    gain_outs = []
    at = 0
    for size in sizes:
        gain_outs.append(gains[at : at + size])
        at += size
    return (
        output,
        grad_tokens,
        *gain_outs,
        attn_grad[:, :query_cols].astype(jnp.float32),
        attn_grad[:, query_cols : query_cols + key_cols].astype(jnp.float32),
        attn_grad[:, query_cols + key_cols : query_cols + 2 * key_cols].astype(jnp.float32),
        attn_grad[:, query_cols + 2 * key_cols :].astype(jnp.float32).T,
        grad_feed_w[:, :hidden_cols],
        grad_feed_w[:, hidden_cols : 2 * hidden_cols],
        grad_feed_w[:, 2 * hidden_cols :].T,
    )


def solution(mesh):
    in_specs = (
        P("dp", None, "tensor", None),
        P("dp", None, "tensor", None),
        P(),
        P(),
        P(),
        P(),
        P(),
        P(),
        P(),
        P("dp", "tensor"),
        P("dp", "tensor"),
        P("dp", "tensor"),
        P("tensor", "dp"),
        P("dp", "tensor"),
        P("dp", "tensor"),
        P("tensor", "dp"),
    )
    out_specs = (
        P("dp", None, "tensor", None),
        P("dp", None, "tensor", None),
        P(),
        P(),
        P(),
        P(),
        P("dp", "tensor"),
        P("dp", "tensor"),
        P("dp", "tensor"),
        P("tensor", "dp"),
        P("dp", "tensor"),
        P("dp", "tensor"),
        P("tensor", "dp"),
    )
    return jax.shard_map(
        on_device, mesh=mesh, in_specs=in_specs, out_specs=out_specs, check_vma=False
    )
```

```python
import jax
import jax.numpy as jnp
from jax import lax
from jax.sharding import PartitionSpec as P

BLOCK = 128
QROWS = 512


EPS = 1e-05
THETA = 1000000.0
NEG = -1e30


def norm_rows(values, gain):
    return values * lax.rsqrt(jnp.mean(values * values, axis=-1, keepdims=True) + EPS) * gain


def norm_pull(values, gain, grad):
    inverse = lax.rsqrt(jnp.mean(values * values, axis=-1, keepdims=True) + EPS)
    scaled = grad * gain
    inner = jnp.mean(values * scaled, axis=-1, keepdims=True)
    grad_values = inverse * scaled - values * (inverse * inverse * inverse * inner)
    return grad_values, jnp.sum(grad * values * inverse, axis=0)


def turn_half(values):
    half = values.shape[-1] // 2
    return jnp.concatenate([-values[..., half:], values[..., :half]], axis=-1)


def rotated(values, gain, cosine, sine):
    normed = norm_rows(values, gain)
    return normed * cosine + turn_half(normed) * sine


def after(values, *others):
    return lax.optimization_barrier((values, others))[0]


def swap(values, axis, bit):
    count = lax.axis_size(axis)
    return lax.ppermute(values, axis, [(index, index ^ bit) for index in range(count)])


def bits_of(count):
    bits = []
    bit = 1
    while bit < count:
        bits.append(bit)
        bit *= 2
    return bits


def dot(left, right):
    return jnp.dot(left, right, preferred_element_type=jnp.float32)


def dot_t(left, right):
    return lax.dot_general(
        left, right, (((1,), (1,)), ((), ())), preferred_element_type=jnp.float32
    )


def dot_tl(left, right):
    return lax.dot_general(
        left, right, (((0,), (0,)), ((), ())), preferred_element_type=jnp.float32
    )


def spread(pieces, axis, bits):
    pieces = dict(pieces)
    for bit in bits:
        for key in sorted(pieces):
            pieces[key | bit] = swap(pieces[key], axis, bit)
    return pieces


def fold(pieces, axis, bits, arrived=None):
    pieces = dict(pieces)
    for bit in bits:
        for key in sorted(pieces, reverse=True):
            if key & bit:
                got = swap(pieces.pop(key).astype(jnp.bfloat16), axis, bit)
                if arrived is not None:
                    arrived.append(got)
                pieces[key ^ bit] = pieces[key ^ bit] + got.astype(jnp.float32)
    return pieces


def widen(values, index, axis, bit, at):
    got = swap(values, axis, bit)
    upper = (index & bit) != 0
    return jnp.stack([jnp.where(upper, got, values), jnp.where(upper, values, got)], axis=at)


def halve(values, index, axis, bit):
    size = values.shape[0] // 2
    mine = ((index & bit) != 0).astype(jnp.int32)
    keep = lax.dynamic_slice_in_dim(values, mine * size, size, 0)
    send = lax.dynamic_slice_in_dim(values, (1 - mine) * size, size, 0)
    got = swap(send, axis, bit)
    return (keep.astype(jnp.float32) + got.astype(jnp.float32)).astype(jnp.bfloat16)


def on_device(
    tokens,
    cotangent,
    lengths,
    groups,
    offsets,
    attention_gain,
    feed_gain,
    query_gain,
    key_gain,
    query_weight,
    key_weight,
    value_weight,
    out_weight,
    gate_weight,
    up_weight,
    down_weight,
):
    shard_shape = tokens.shape
    units, unit, width = shard_shape[1:]
    tensor_count = lax.axis_size("tensor")
    dp_count = lax.axis_size("dp")
    tensor_at = lax.axis_index("tensor")
    group = lax.axis_index("dp")
    far = tensor_count // 2
    local_rows = units * unit
    group_rows = local_rows * tensor_count
    head_dim = query_gain.shape[0]
    tensor_bits = bits_of(tensor_count)
    near_bits = tensor_bits[:-1]
    dp_bits = bits_of(dp_count)
    low = jnp.bfloat16
    query_cols = query_weight.shape[1]
    key_cols = key_weight.shape[1]
    heads = query_cols // head_dim
    value_heads = key_cols // head_dim
    repeat = heads // value_heads
    hidden_cols = gate_weight.shape[1]

    def rows_of_group(block):
        pieces = spread({0: block.reshape(units, 1, unit, width)}, "tensor", tensor_bits[::-1])
        whole = jnp.concatenate([pieces[key] for key in range(tensor_count)], axis=1)
        return whole.reshape(group_rows, width)

    def group_slice(whole, key):
        cols = whole.shape[-1]
        part = whole.reshape(units, tensor_count, unit, cols)[:, key]
        return part.reshape(local_rows, cols)

    def row_blocks(block):
        pieces = spread({0: block}, "tensor", tensor_bits[::-1])
        near = jnp.concatenate([pieces[key] for key in range(far)], axis=0)
        distant = jnp.concatenate([pieces[key] for key in range(far, tensor_count)], axis=0)
        return near, distant

    def block_of(near, distant, key):
        half = near if key < far else distant
        at = (key % far) * local_rows
        return lax.slice_in_dim(half, at, at + local_rows, axis=0)

    def sum_to_rows(make, between):
        distant = {key - far: make(key) for key in range(2 * far - 1, far - 1, -1)}
        distant = fold(distant, "tensor", near_bits)[0]
        pieces = {key: make(key) for key in range(far - 1, -1, -1)}
        send = after(distant.astype(low), *between())
        pieces = {key: after(piece, send) for key, piece in pieces.items()}
        got = swap(send, "tensor", far).astype(jnp.float32)
        arrived = []
        near = fold(pieces, "tensor", near_bits, arrived)[0]
        return near + got, arrived, send

    def whole_weight(shard):
        return lax.all_gather(shard, "dp", axis=0, tiled=True)

    def weight_grad(whole):
        return lax.psum_scatter(whole.astype(low), "dp", scatter_dimension=0, tiled=True)

    local_x = tokens.reshape(local_rows, width).astype(jnp.float32)
    attn_rows = rows_of_group(norm_rows(local_x, attention_gain).astype(low))
    attn_pack = jnp.concatenate([query_weight, key_weight, value_weight, out_weight.T], axis=1)
    attn_cols = attn_pack.shape[1]
    for bit in dp_bits[1:-1]:
        attn_pack = widen(attn_pack, group, "dp", bit, 0)
    attn_pack = widen(attn_pack, group, "dp", 1, attn_pack.ndim - 2)
    attn_pack = widen(attn_pack, group, "dp", dp_bits[-1], 0).reshape(width, attn_cols)
    project = attn_pack[:, : query_cols + 2 * key_cols]
    out_turned = attn_pack[:, query_cols + 2 * key_cols :]
    feed_pack = whole_weight(jnp.concatenate([gate_weight, up_weight, down_weight.T], axis=1))
    gate_full = feed_pack[:, :hidden_cols]
    up_full = feed_pack[:, hidden_cols : 2 * hidden_cols]
    down_full = feed_pack[:, 2 * hidden_cols :]
    local_back = cotangent.reshape(local_rows, width)
    back_near, back_far = row_blocks(after(local_back, attn_rows))
    back_rows = jnp.concatenate([back_near, back_far], axis=0)

    row = jnp.arange(group_rows, dtype=jnp.int32)
    relative = (row // unit) % tensor_count
    position = row + ((relative ^ tensor_at) - relative) * unit
    start = offsets * BLOCK
    finish = start + lengths
    number = jnp.arange(lengths.shape[0], dtype=jnp.int32)
    inside = (
        (groups[None, :] == group)
        & (position[:, None] >= start[None, :])
        & (position[:, None] < finish[None, :])
    ).astype(jnp.int32)
    segment = jnp.sum(inside * (number + 1)[None, :], axis=1) - 1
    segment = jnp.where(segment >= 0, segment, -1 - position)
    inner_pos = jnp.sum(inside * (position[:, None] - start[None, :]), axis=1)
    freq = THETA ** (-(jnp.arange(head_dim // 2, dtype=jnp.float32) * 2.0) / head_dim)
    angle = inner_pos.astype(jnp.float32)[:, None] * freq[None, :]
    cosine = jnp.concatenate([jnp.cos(angle), jnp.cos(angle)], axis=1)[:, None, :]
    sine = jnp.concatenate([jnp.sin(angle), jnp.sin(angle)], axis=1)[:, None, :]

    projected = dot(attn_rows, project)
    query_pre = projected[:, :query_cols].reshape(group_rows, heads, head_dim)
    key_pre = projected[:, query_cols : query_cols + key_cols].reshape(
        group_rows, value_heads, head_dim
    )
    value_pre = projected[:, query_cols + key_cols :]
    queries = (
        rotated(query_pre, query_gain, cosine, sine)
        .astype(jnp.bfloat16)
        .reshape(group_rows, value_heads, repeat, head_dim)
    )
    keys = rotated(key_pre, key_gain, cosine, sine).astype(jnp.bfloat16)
    values = value_pre.astype(jnp.bfloat16).reshape(group_rows, value_heads, head_dim)
    scale = head_dim ** (-0.5)
    block_count = group_rows // QROWS

    def block_scores(index):
        first = index * QROWS
        last = first + QROWS
        scores = (
            jnp.einsum(
                "qkgd,pkd->kgqp",
                queries[first:last],
                keys[:last],
                preferred_element_type=jnp.float32,
            )
            * scale
        )
        allowed = (segment[first:last, None] == segment[None, :last]) & (
            position[None, :last] <= position[first:last, None]
        )
        return jnp.where(allowed, scores, NEG)

    mixed_parts = []
    log_totals = []
    for index in range(block_count):
        last = (index + 1) * QROWS
        scores = block_scores(index)
        summit = jnp.max(scores, axis=-1, keepdims=True)
        shifted = jnp.exp(scores - summit)
        total = jnp.sum(shifted, axis=-1, keepdims=True)
        attend = (shifted / total).astype(jnp.bfloat16)
        log_totals.append(summit + jnp.log(total))
        mixed_parts.append(
            jnp.einsum("kgqp,pkd->qkgd", attend, values[:last], preferred_element_type=jnp.float32)
        )
    mixed = (
        jnp.concatenate(mixed_parts, axis=0)
        .reshape(group_rows, heads * head_dim)
        .astype(jnp.bfloat16)
    )
    mixed = after(mixed, back_near, back_far)
    attn_out, _, _ = sum_to_rows(
        lambda key: dot_t(group_slice(mixed, key), out_turned), lambda: ()
    )
    attn_out = after(attn_out, feed_pack)
    middle = local_x + attn_out
    feed_near, feed_far = row_blocks(norm_rows(middle, feed_gain).astype(low))

    def feed(rows, back):
        gate = dot(rows, gate_full)
        up = dot(rows, up_full)
        grad_hidden = dot(back, down_full)
        sigmoid = jax.nn.sigmoid(gate)
        silu = gate * sigmoid
        hidden = (silu * up).astype(low)
        grad_gate = (grad_hidden * up * sigmoid * (1.0 + gate * (1.0 - sigmoid))).astype(low)
        grad_up = (grad_hidden * silu).astype(low)
        return hidden, grad_gate, grad_up

    near_parts = feed(feed_near, back_near)
    far_parts = feed(after(feed_far, near_parts), back_far)

    def grad_feed_part(key):
        return dot_t(block_of(near_parts[1], far_parts[1], key), gate_full) + dot_t(
            block_of(near_parts[2], far_parts[2], key), up_full
        )

    grad_feed_in, _, _ = sum_to_rows(grad_feed_part, lambda: ())
    hidden, grad_gate, grad_up = (
        jnp.concatenate([one, two], axis=0) for one, two in zip(near_parts, far_parts)
    )
    feed_rows = jnp.concatenate([feed_near, feed_far], axis=0)
    hidden, grad_gate, grad_up = after((hidden, grad_gate, grad_up), grad_feed_in)
    grad_feed_pack = jnp.concatenate(
        [
            dot_tl(feed_rows, grad_gate).astype(low),
            dot_tl(feed_rows, grad_up).astype(low),
            dot_tl(back_rows, hidden).astype(low),
        ],
        axis=1,
    )
    grad_feed_w = weight_grad(grad_feed_pack).astype(jnp.float32)
    grad_middle_norm, grad_feed_gain = norm_pull(middle, feed_gain, grad_feed_in)
    grad_middle = local_back.astype(jnp.float32) + grad_middle_norm
    back_attn = rows_of_group(grad_middle.astype(low))
    back_attn = after(back_attn, grad_feed_pack)
    grad_out_turned = dot_tl(back_attn, mixed).astype(low)
    grad_mixed = (
        dot(back_attn, out_turned)
        .astype(low)
        .reshape(group_rows, value_heads, repeat, head_dim)
    )
    grad_keys = jnp.zeros((group_rows, value_heads, head_dim), jnp.float32)
    grad_values = jnp.zeros((group_rows, value_heads, head_dim), jnp.float32)
    query_parts = []
    for index in range(block_count - 1, -1, -1):
        first = index * QROWS
        last = first + QROWS
        scores = block_scores(index)
        attend = jnp.exp(scores - log_totals[index])
        attend_low = attend.astype(jnp.bfloat16)
        grad_here = grad_mixed[first:last]
        grad_values = grad_values.at[:last].add(
            jnp.einsum("kgqp,qkgd->pkd", attend_low, grad_here, preferred_element_type=jnp.float32)
        )
        grad_attend = jnp.einsum(
            "qkgd,pkd->kgqp", grad_here, values[:last], preferred_element_type=jnp.float32
        )
        inner = jnp.sum(attend * grad_attend, axis=-1, keepdims=True)
        grad_scores = (attend * (grad_attend - inner)).astype(jnp.bfloat16)
        if index == block_count - 1:
            first_block = grad_scores
        query_parts.append(
            jnp.einsum(
                "kgqp,pkd->qkgd", grad_scores, keys[:last], preferred_element_type=jnp.float32
            )
            * scale
        )
        grad_keys = grad_keys.at[:last].add(
            jnp.einsum(
                "kgqp,qkgd->pkd",
                grad_scores,
                queries[first:last],
                preferred_element_type=jnp.float32,
            )
            * scale
        )
    query_parts = query_parts[::-1]
    feed_out, feed_arrived, feed_sent = sum_to_rows(
        lambda key: dot_t(
            lax.slice_in_dim(hidden, key * local_rows, (key + 1) * local_rows, axis=0), down_full
        ),
        lambda: (first_block,),
    )
    output = (middle + feed_out).astype(low).reshape(shard_shape)
    grad_queries = jnp.concatenate(query_parts, axis=0).reshape(group_rows, heads, head_dim)

    def query_side(values_in, gain_in):
        return rotated(values_in, gain_in, cosine, sine)

    _, query_pull = jax.vjp(query_side, query_pre, query_gain)
    grad_query_pre, grad_query_gain = query_pull(grad_queries)
    _, key_pull = jax.vjp(query_side, key_pre, key_gain)
    grad_key_pre, grad_key_gain = key_pull(grad_keys)
    grad_project = jnp.concatenate(
        [
            grad_query_pre.reshape(group_rows, query_cols),
            grad_key_pre.reshape(group_rows, key_cols),
            grad_values.reshape(group_rows, key_cols),
        ],
        axis=1,
    ).astype(jnp.bfloat16)
    grad_project = after(grad_project, feed_arrived)
    later = {}

    def grad_rows_part(key):
        part = dot_t(group_slice(grad_project, key), project)
        if key == 2 * far - 1:
            later["project"] = after(grad_project, part)
        return part

    def tail_between():
        full = dot_tl(attn_rows, later["project"])
        grad_attention_gain = jnp.sum(full * project.astype(jnp.float32), axis=1) / attention_gain
        pack = jnp.concatenate([full.astype(low), grad_out_turned], axis=1)
        gains = jnp.concatenate(
            [grad_attention_gain, grad_feed_gain, grad_query_gain, grad_key_gain]
        )
        later["gains"] = gains
        later["sums"] = halve(pack, group, "dp", dp_bits[-1])
        return grad_feed_w, output

    grad_attn_in, arrived, _ = sum_to_rows(grad_rows_part, tail_between)
    gains, attn_grad = after((later["gains"], later["sums"]), arrived)
    for bit in tensor_bits:
        gains = gains + swap(gains, "tensor", bit)
    for bit in dp_bits[::-1]:
        gains = gains + swap(gains, "dp", bit)
    for bit in dp_bits[-2::-1]:
        attn_grad = halve(attn_grad, group, "dp", bit)
    grad_x_norm, _ = norm_pull(local_x, attention_gain, grad_attn_in)
    grad_tokens = (grad_middle + grad_x_norm).astype(low).reshape(shard_shape)
    sizes = (width, width, head_dim, head_dim)
    gain_outs = []
    at = 0
    for size in sizes:
        gain_outs.append(gains[at : at + size])
        at += size
    return (
        output,
        grad_tokens,
        *gain_outs,
        attn_grad[:, :query_cols].astype(jnp.float32),
        attn_grad[:, query_cols : query_cols + key_cols].astype(jnp.float32),
        attn_grad[:, query_cols + key_cols : query_cols + 2 * key_cols].astype(jnp.float32),
        attn_grad[:, query_cols + 2 * key_cols :].astype(jnp.float32).T,
        grad_feed_w[:, :hidden_cols],
        grad_feed_w[:, hidden_cols : 2 * hidden_cols],
        grad_feed_w[:, 2 * hidden_cols :].T,
    )


def solution(mesh):
    in_specs = (
        P("dp", None, "tensor", None),
        P("dp", None, "tensor", None),
        P(),
        P(),
        P(),
        P(),
        P(),
        P(),
        P(),
        P("dp", "tensor"),
        P("dp", "tensor"),
        P("dp", "tensor"),
        P("tensor", "dp"),
        P("dp", "tensor"),
        P("dp", "tensor"),
        P("tensor", "dp"),
    )
    out_specs = (
        P("dp", None, "tensor", None),
        P("dp", None, "tensor", None),
        P(),
        P(),
        P(),
        P(),
        P("dp", "tensor"),
        P("dp", "tensor"),
        P("dp", "tensor"),
        P("tensor", "dp"),
        P("dp", "tensor"),
        P("dp", "tensor"),
        P("tensor", "dp"),
    )
    return jax.shard_map(
        on_device, mesh=mesh, in_specs=in_specs, out_specs=out_specs, check_vma=False
    )
```
